256 devices in a mesh: grp: 8 (over x, core), dev: 32 (over z, y).
Axes of the slice: x: 4, y: 4, z: 8, core: 2. Of those that a mesh axis runs over, the one named last changes fastest.
Arguments:
- right_side: float32 [24576, 512], P(('grp', 'dev')), may hold values from -6 to 6
- ghost_rows: int32 [512, 24], P(('grp', 'dev')), may hold values from 0 to 95
- cols_one: int32 [24576, 2], P(('grp', 'dev')), may hold values from 0 to 143
- diag_one: float32 [24576, 4096], P(('grp', 'dev')), may hold values from -1 to 7
- offd_one: float32 [24576, 2, 4096], P(('grp', 'dev')), may hold values from -0.75 to 0.75
- prol_one: float32 [24576, 4096], P(('grp', 'dev')), may hold values from -0.75 to 0.75
- agg_one: int32 [24576], P(('grp', 'dev')), may hold values from 0 to 95
- cols_two: int32 [12288, 2], P(('grp', 'dev')), may hold values from 0 to 287, as said below
- diag_two: float32 [12288, 4096], P(('grp', 'dev')), may hold values from -1 to 7
- offd_two: float32 [12288, 2, 4096], P(('grp', 'dev')), may hold values from -0.75 to 0.75
- prol_two: float32 [12288, 4096], P(('grp', 'dev')), may hold values from -0.375 to 0.375
- agg_two: int32 [12288], P(('grp', 'dev')), may hold values from 0 to 31
- cols_three: int32 [32, 2], replicated, may hold values from 0 to 31
- diag_three: float32 [32, 4096], replicated, may hold values from -1 to 7
- offd_three: float32 [32, 2, 4096], replicated, may hold values from -0.75 to 0.75
Outputs:
- solution: float32 [24576, 512], P(('grp', 'dev'))
- coarse_solution: float32 [32, 512], replicated
The draws below stay inside these ranges and needn't reach their ends.
Inputs may be any that keep to these rules, and one draw needn't show every extreme that they name: `cols_two`: columns k = 0, 2, 4, ... read only pair blocks p - 1 and p (values below 192); columns k = 1, 3, 5, ... read only pair blocks p and p + 1 (values from 96 on).
All inputs are finite; a program needn't handle non-finite values.
Results may differ from the reference program's by a relative error of at most 0.00011.
Values sent between devices are 32-bit elements; how exact they have to be, the bound alone decides.
No kernel may reach another device: no remote copies, remote signals or barrier semaphores. Data moves between devices by JAX's collectives and lax.ppermute only.
A program may use at most 128 MiB of HBM per device.

```python
import jax
import jax.numpy as jnp
from jax import lax

TILE = 64
LOADS = 8
ROWS = 96
OFFD = 2
COARSE = 32
DEGREE = 3
COARSE_DEGREE = 8
GHOST = 24
BLOCKS = 256
PAIRS = 128
ROWS_ALL = 24576
HALF_ALL = 12288


def dominant_tiles(key, row_count):
    flat_index = jnp.arange(TILE * TILE)
    on_diagonal = (flat_index % (TILE + 1) == 0).astype(jnp.float32)
    scale_key, dense_key = jax.random.split(key)
    diag_level = jax.random.uniform(scale_key, (row_count, 1), jnp.float32, 3.2, 6.4)
    dense_part = jnp.clip(jax.random.normal(dense_key, (row_count, TILE * TILE), jnp.float32), -4.0, 4.0)
    return diag_level * on_diagonal + dense_part * (0.35 / TILE ** 0.5)


def draw_diag_one(key, part):
    return dominant_tiles(jax.random.fold_in(key, 11), ROWS_ALL)


def draw_diag_two(key, part):
    return dominant_tiles(jax.random.fold_in(key, 23), HALF_ALL)


def draw_diag_three(key, part):
    return dominant_tiles(jax.random.fold_in(key, 37), COARSE)


def draw_cols_two(key, part):
    offsets = jax.random.randint(jax.random.fold_in(key, 41), (HALF_ALL, OFFD), 0, 2 * ROWS, jnp.int32)
    sides = jnp.arange(OFFD, dtype=jnp.int32) % 2 * ROWS
    return offsets + sides[None, :]


def plant(values, stream_key, smallest, high):
    shape = values.shape
    index_at = [jax.random.randint(jax.random.fold_in(stream_key, axis), (), 0, shape[axis]) for axis in range(len(shape))]
    values = values.at[tuple(index_at)].set(smallest)
    longest = shape.index(max(shape))
    index_at[longest] = (index_at[longest] + 1) % shape[longest]
    return values.at[tuple(index_at)].set(high)


def steps_of(own_key, dims, pieces, least, top_value):
    level, own = 1.0, jax.random.fold_in(own_key, 6)
    for dim, blocks in pieces:
        draws = jnp.exp(jax.random.uniform(jax.random.fold_in(own, dim), (blocks,), jnp.float32, least / len(pieces), top_value / len(pieces)))
        level = level * jnp.repeat(draws, dims[dim] // blocks).reshape([-1 if axis == dim else 1 for axis in range(len(dims))])
    return level


def gaussian(key, shape, deviation, reach, shards=(), kind=jnp.bfloat16):
    values = deviation * jax.random.normal(key, shape, jnp.float32)
    if shards:
        values = values * steps_of(key, shape, shards, -0.22, 0.18)
    return jnp.clip(values, -reach, reach).astype(kind)


def setup_inputs(seed: int = 0) -> dict:
    seeds = jax.random.split(jax.random.key(seed), 16)
    right_side = gaussian(seeds[0], (ROWS_ALL, LOADS * TILE), 1.0, 6.0, ((0, 256),), jnp.float32)
    ghost_rows = plant(jax.random.randint(seeds[1], (2 * BLOCKS, GHOST), 0, ROWS), jax.random.fold_in(seeds[1], 1), 0, ROWS - 1).astype(jnp.int32)
    cols_one = plant(jax.random.randint(seeds[2], (ROWS_ALL, OFFD), 0, ROWS + 2 * GHOST), jax.random.fold_in(seeds[2], 1), 0, (ROWS + 2 * GHOST) - 1).astype(jnp.int32)
    diag_one = draw_diag_one(jax.random.fold_in(seeds[15], 71), 0)
    offd_one = gaussian(seeds[4], (ROWS_ALL, OFFD, TILE * TILE), TILE ** -0.5, 0.75, ((0, 256),), jnp.float32)
    prol_one = gaussian(seeds[5], (ROWS_ALL, TILE * TILE), TILE ** -0.5, 0.75, ((0, 256),), jnp.float32)
    agg_one = plant(jax.random.randint(seeds[6], (ROWS_ALL,), 0, ROWS), jax.random.fold_in(seeds[6], 1), 0, ROWS - 1).astype(jnp.int32)
    cols_two = draw_cols_two(jax.random.fold_in(seeds[15], 71), 0)
    diag_two = draw_diag_two(jax.random.fold_in(seeds[15], 71), 0)
    offd_two = gaussian(seeds[9], (HALF_ALL, OFFD, TILE * TILE), TILE ** -0.5, 0.75, ((0, 256),), jnp.float32)
    prol_two = gaussian(seeds[10], (HALF_ALL, TILE * TILE), (4 * TILE) ** -0.5, 0.375, ((0, 256),), jnp.float32)
    agg_two = plant(jax.random.randint(seeds[11], (HALF_ALL,), 0, COARSE), jax.random.fold_in(seeds[11], 1), 0, COARSE - 1).astype(jnp.int32)
    cols_three = plant(jax.random.randint(seeds[12], (COARSE, OFFD), 0, COARSE), jax.random.fold_in(seeds[12], 1), 0, COARSE - 1).astype(jnp.int32)
    diag_three = draw_diag_three(jax.random.fold_in(seeds[15], 71), 0)
    offd_three = gaussian(seeds[14], (COARSE, OFFD, TILE * TILE), TILE ** -0.5, 0.75, (), jnp.float32)
    return {"right_side": right_side, "ghost_rows": ghost_rows, "cols_one": cols_one, "diag_one": diag_one, "offd_one": offd_one, "prol_one": prol_one, "agg_one": agg_one, "cols_two": cols_two, "diag_two": diag_two, "offd_two": offd_two, "prol_two": prol_two, "agg_two": agg_two, "cols_three": cols_three, "diag_three": diag_three, "offd_three": offd_three}


cheb_low = 1.0
cheb_high = 9.0
highest = lax.Precision.HIGHEST


def as_tiles(flat_tile):
    return flat_tile.reshape(flat_tile.shape[:-1] + (TILE, TILE))


def apply_tiles(diag_part, offd_part, own_rows, picked):
    own_rows = own_rows.reshape(own_rows.shape[0], LOADS, TILE)
    picked = picked.reshape(picked.shape[0], picked.shape[1], LOADS, TILE)
    result = jnp.einsum("iab,ivb->iva", as_tiles(diag_part), own_rows, precision=highest)
    result = result + jnp.einsum("ikab,ikvb->iva", as_tiles(offd_part), picked, precision=highest)
    return result.reshape(result.shape[0], LOADS * TILE)


def prolong(prol, coarse_rows):
    coarse_rows = coarse_rows.reshape(coarse_rows.shape[0], LOADS, TILE)
    result = jnp.einsum("iab,ivb->iva", as_tiles(prol), coarse_rows, precision=highest)
    return result.reshape(result.shape[0], LOADS * TILE)


def transposed(prol, fine_rows):
    fine_rows = fine_rows.reshape(fine_rows.shape[0], LOADS, TILE)
    result = jnp.einsum("iab,iva->ivb", as_tiles(prol), fine_rows, precision=highest)
    return result.reshape(result.shape[0], LOADS * TILE)


def chebyshev(operate, solution, residual, degree, finish):
    center = 0.5 * (cheb_high + cheb_low)
    radius = 0.5 * (cheb_high - cheb_low)
    sigma_value = center / radius
    rho_now = 1.0 / sigma_value
    direction = residual / center
    solution = solution + direction
    for turn_index in range(degree - 1):
        residual = residual - operate(direction)
        rho_next = 1.0 / (2.0 * sigma_value - rho_now)
        direction = (rho_next * rho_now) * direction + (2.0 * rho_next / radius) * residual
        solution = solution + direction
        rho_now = rho_next
    if finish:
        residual = residual - operate(direction)
    return solution, residual


def pick_rows(source, index_rows):
    return source[index_rows]


def reference(right_side, ghost_rows, cols_one, diag_one, offd_one, prol_one, agg_one, cols_two, diag_two, offd_two, prol_two, agg_two, cols_three, diag_three, offd_three):
    width = LOADS * TILE
    pick = jax.vmap(pick_rows)

    def level_one(vector):
        blocks = vector.reshape(BLOCKS, ROWS, width)
        zero_block = jnp.zeros_like(blocks[:1])
        left_blocks = jnp.concatenate([zero_block, blocks[:-1]], 0)
        right_blocks = jnp.concatenate([blocks[1:], zero_block], 0)
        lists = ghost_rows.reshape(BLOCKS, 2, GHOST)
        windows = jnp.concatenate([pick(left_blocks, lists[:, 0]), blocks, pick(right_blocks, lists[:, 1])], 1)
        picked = pick(windows, cols_one.reshape(BLOCKS, ROWS * OFFD)).reshape(ROWS_ALL, OFFD, width)
        return apply_tiles(diag_one, offd_one, vector, picked)

    def level_two(vector):
        pairs = vector.reshape(PAIRS, ROWS, width)
        zero_pair = jnp.zeros_like(pairs[:1])
        left_pairs = jnp.concatenate([zero_pair, pairs[:-1]], 0)
        right_pairs = jnp.concatenate([pairs[1:], zero_pair], 0)
        windows = jnp.concatenate([left_pairs, pairs, right_pairs], 1)
        picked = pick(windows, cols_two.reshape(PAIRS, ROWS * OFFD)).reshape(HALF_ALL, OFFD, width)
        return apply_tiles(diag_two, offd_two, vector, picked)

    def level_three(vector):
        return apply_tiles(diag_three, offd_three, vector, vector[cols_three])

    smooth_one, res_one = chebyshev(level_one, jnp.zeros_like(right_side), right_side, DEGREE, True)
    terms_one = transposed(prol_one, res_one).reshape(PAIRS, 2 * ROWS, width)
    pair_agg = agg_one.reshape(PAIRS, 2 * ROWS)
    one_hot = (pair_agg[:, None, :] == jnp.arange(ROWS, dtype=jnp.int32)[None, :, None]).astype(jnp.float32)
    rhs_two = jnp.einsum("pgi,piw->pgw", one_hot, terms_one, precision=highest).reshape(HALF_ALL, width)

    smooth_two, res_two = chebyshev(level_two, jnp.zeros_like(rhs_two), rhs_two, DEGREE, True)
    terms_two = transposed(prol_two, res_two)
    coarse_hot = (agg_two[None, :] == jnp.arange(COARSE, dtype=jnp.int32)[:, None]).astype(jnp.float32)
    coarse_rhs = jnp.dot(coarse_hot, terms_two, precision=highest)

    coarse_solution = chebyshev(level_three, jnp.zeros_like(coarse_rhs), coarse_rhs, COARSE_DEGREE, False)[0]

    corrected_two = smooth_two + prolong(prol_two, coarse_solution[agg_two])
    smoothed_two = chebyshev(level_two, corrected_two, rhs_two - level_two(corrected_two), DEGREE, False)[0]

    pair_rows = jnp.repeat(smoothed_two.reshape(PAIRS, ROWS, width), 2, axis=0)
    lifted = pick(pair_rows, agg_one.reshape(BLOCKS, ROWS)).reshape(ROWS_ALL, width)
    corrected_one = smooth_one + prolong(prol_one, lifted)
    solution = chebyshev(level_one, corrected_one, right_side - level_one(corrected_one), DEGREE, False)[0]
    return solution, coarse_solution
```

```python
import functools

import jax
import jax.numpy as jnp
from jax import lax
from jax.experimental import pallas as pl
from jax.experimental.pallas import tpu as pltpu
from jax.sharding import PartitionSpec as P

TILE = 64
LOADS = 8
ROWS = 96
HALF = 48
COARSE = 32
GHOST = 24
AXES = ("grp", "dev")

CENTER = 5.0
RADIUS = 4.0
SIGMA = 1.25

bf16 = jnp.bfloat16
f32 = jnp.float32
VM = pl.BlockSpec(memory_space=pltpu.VMEM)
SM = pl.BlockSpec(memory_space=pltpu.SMEM)


def chebyshev_factors(count):
    rho = 1.0 / SIGMA
    factors = []
    for _ in range(count):
        rho_next = 1.0 / (2.0 * SIGMA - rho)
        factors.append((rho_next * rho, 2.0 * rho_next / RADIUS))
        rho = rho_next
    return factors


FACTORS = chebyshev_factors(7)


def low_lanes(shape):
    return lax.broadcasted_iota(jnp.int32, shape, len(shape) - 1) < TILE


def swap(value):
    return pltpu.roll(value, TILE, value.ndim - 1)


def split(value):
    high = value.astype(bf16)
    return high, (value - high.astype(f32)).astype(bf16)


def dot_nt(a, b):
    return lax.dot_general(a, b, (((1,), (1,)), ((), ())), preferred_element_type=f32)


def dot_nn(a, b):
    return lax.dot_general(a, b, (((1,), (0,)), ((), ())), preferred_element_type=f32)


def fill_table(table, start, count, base, read):
    def step(q, _):
        value = read(q)
        table[start + q] = value
        table[base + start + q] = swap(value)
        return 0

    lax.fori_loop(0, count, step, 0, unroll=4)


def block_products(left, high_w, low_w):
    high, low = split(left)
    both = dot_nt(jnp.concatenate([high, low], 0), high_w)
    rest = dot_nt(high, low_w)
    mask = low_lanes((8, 128))

    def block(i):
        lanes = slice((i // 2) * 128, (i // 2) * 128 + 128)
        return (
            both[8 * i : 8 * i + 8, lanes]
            + both[32 + 8 * i : 40 + 8 * i, lanes]
            + rest[8 * i : 8 * i + 8, lanes]
        )

    return [jnp.where(mask, block(2 * j), block(2 * j + 1)) for j in range(2)]


def operator_group(table, base, own, g, index_ref, count, high_ref, low_ref):
    mask = low_lanes((8, 128))
    rows = []
    for i in range(4):
        mine = table[(i & 1) * base + own + 2 * g + (i >> 1)]
        first = table[index_ref[4 * g + i]]
        second = table[index_ref[count + 4 * g + i]]
        rows.append(jnp.concatenate([jnp.where(mask, mine, first), second], 1))
    left = jnp.concatenate(rows, 0)
    at = pl.ds(pl.multiple_of(g * 256, 256), 256)
    return block_products(left, high_ref[at, :], low_ref[at, :])


def prolong_group(table, base, g, index_ref, high_ref, low_ref, row_start):
    rows = [table[index_ref[row_start + 4 * g + i]] for i in range(4)]
    left = jnp.concatenate(rows, 0)
    at = pl.ds(pl.multiple_of(g * 256, 256), 256)
    return block_products(left, high_ref[at, :], low_ref[at, :])


def restrict_group(pair0, pair1, g, agg_ref, high_ref, low_ref, sums):
    mask = low_lanes((8, 128))
    zero = jnp.zeros((8, 128), f32)
    rows = [
        jnp.concatenate([jnp.where(mask, pair0, zero), zero], 1),
        jnp.concatenate([jnp.where(mask, zero, pair0), zero], 1),
        jnp.concatenate([zero, jnp.where(mask, pair1, zero)], 1),
        jnp.concatenate([zero, jnp.where(mask, zero, pair1)], 1),
    ]
    high, low = split(jnp.concatenate(rows, 0))
    at = pl.ds(pl.multiple_of(g * 256, 256), 256)
    high_w, low_w = high_ref[at, :], low_ref[at, :]
    both = dot_nn(jnp.concatenate([high, low], 0), high_w)
    terms = both[:32] + both[32:] + dot_nn(high, low_w)
    for i in range(4):
        row = agg_ref[4 * g + i]
        sums[row] = sums[row] + terms[8 * i : 8 * i + 8]


def zero_sums(sums, count):
    def step(q, _):
        sums[q] = jnp.zeros((8, 128), f32)
        return 0

    lax.fori_loop(0, count, step, 0, unroll=8)


def pack_sums(sums, out, count):
    def step(q, _):
        out[q] = sums[2 * q] + swap(sums[2 * q + 1])
        return 0

    lax.fori_loop(0, count // 2, step, 0, unroll=4)


def gather_sends(vector, send_ref, to_left, to_right):
    mask = low_lanes((8, 128))

    def half(row, odd):
        value = vector[row >> 1]
        return jnp.where((row & 1) == odd, value, swap(value))

    def step(q, _):
        for side, out in ((0, to_left), (1, to_right)):
            at = side * GHOST + 2 * q
            out[q] = jnp.where(mask, half(send_ref[at], 0), half(send_ref[at + 1], 1))
        return 0

    lax.fori_loop(0, GHOST // 2, step, 0, unroll=2)


def prepare_operator_kernel(*refs, sources, steps):
    blocks = refs[: 2 * sources]
    high_ref, low_ref, stage_a, stage_b = refs[2 * sources :]
    mask = low_lanes((32, 128))
    zero = jnp.zeros((32, 128), f32)

    def run(diag_ref, offd_ref):
        for i in range(8):
            diag, first, second = diag_ref[i], offd_ref[i, 0], offd_ref[i, 1]
            stage_a[pl.ds(0, 32, stride=2), :] = jnp.where(mask, diag, swap(first))
            stage_a[pl.ds(1, 32, stride=2), :] = jnp.where(mask, swap(diag), first)
            stage_b[pl.ds(0, 32, stride=2), :] = jnp.where(mask, second, zero)
            stage_b[pl.ds(1, 32, stride=2), :] = jnp.where(mask, swap(second), zero)
            for stage, lanes in ((stage_a, slice(0, 128)), (stage_b, slice(128, 256))):
                high, low = split(stage[...])
                high_ref[64 * i : 64 * i + 64, lanes] = high
                low_ref[64 * i : 64 * i + 64, lanes] = low

    if sources == 1:
        run(*blocks)
    else:
        at = pl.program_id(0)
        pl.when(at < steps)(lambda: run(blocks[0], blocks[1]))
        pl.when(at >= steps)(lambda: run(blocks[2], blocks[3]))


def prepare_operator(pairs):
    rows = pairs[0][0].shape[0]
    steps = rows // 8
    sources = len(pairs)
    specs = []
    for s in range(sources):
        place = functools.partial(lambda s, g: jnp.clip(g - s * steps, 0, steps - 1), s)
        specs.append(pl.BlockSpec((8, 32, 128), lambda g, place=place: (place(g), 0, 0)))
        specs.append(pl.BlockSpec((8, 2, 32, 128), lambda g, place=place: (place(g), 0, 0, 0)))
    total = rows * sources
    out = jax.ShapeDtypeStruct((total * TILE, 256), bf16)
    out_spec = pl.BlockSpec((512, 256), lambda g: (g, 0))
    return pl.pallas_call(
        functools.partial(prepare_operator_kernel, sources=sources, steps=steps),
        out_shape=(out, out),
        grid=(steps * sources,),
        in_specs=specs,
        out_specs=(out_spec, out_spec),
        scratch_shapes=[pltpu.VMEM((64, 128), f32), pltpu.VMEM((64, 128), f32)],
        cost_estimate=pl.CostEstimate(
            flops=total * 16384 * 40, bytes_accessed=total * 114688, transcendentals=0
        ),
    )(*[x for pair in pairs for x in pair])


def prepare_transfer_kernel(prol_ref, high_ref, low_ref, stage):
    mask = low_lanes((32, 128))
    zero = jnp.zeros((32, 128), f32)
    for i in range(8):
        prol = prol_ref[i]
        stage[pl.ds(0, 32, stride=2), :] = jnp.where(mask, prol, zero)
        stage[pl.ds(1, 32, stride=2), :] = jnp.where(mask, swap(prol), zero)
        high, low = split(stage[...])
        high_ref[64 * i : 64 * i + 64, :] = high
        low_ref[64 * i : 64 * i + 64, :] = low


def prepare_transfer(prol):
    rows = prol.shape[0]
    out = jax.ShapeDtypeStruct((rows * TILE, 128), bf16)
    out_spec = pl.BlockSpec((512, 128), lambda g: (g, 0))
    return pl.pallas_call(
        prepare_transfer_kernel,
        out_shape=(out, out),
        grid=(rows // 8,),
        in_specs=[pl.BlockSpec((8, 32, 128), lambda g: (g, 0, 0))],
        out_specs=(out_spec, out_spec),
        scratch_shapes=[pltpu.VMEM((64, 128), f32)],
        cost_estimate=pl.CostEstimate(
            flops=rows * 8192 * 20, bytes_accessed=rows * 49152, transcendentals=0
        ),
    )(prol)


def unpack_natural(source, rows_by_load, scale):
    mask = low_lanes((ROWS, 128))
    for t in range(4):
        value = source[:, 128 * t : 128 * t + 128] * scale
        other = swap(value)
        rows_by_load[pl.ds(2 * t, ROWS, stride=8), :] = jnp.where(mask, value, other)
        rows_by_load[pl.ds(2 * t + 1, ROWS, stride=8), :] = jnp.where(mask, other, value)


def update_step(q, product, residual_in, direction_in, solution_in, factors, outs):
    residual = residual_in - product
    if factors is None:
        direction = residual / CENTER
    else:
        direction = factors[0] * direction_in + factors[1] * residual
    outs[0][q] = residual
    outs[1][q] = direction
    outs[2][q] = solution_in + direction


def first_one_kernel(
    flags, ghosts, index_ref, send_ref, mine, left, right, high_ref, low_ref,
    rhs_out, r_out, d_out, x_out, to_left, to_right, table, by_load,
):
    base = 72
    mask = low_lanes((8, 128))

    def row(r):
        return by_load[pl.ds(pl.multiple_of(8 * r, 8), 8), :]

    unpack_natural(mine, by_load, 1.0)

    def own(q):
        value = jnp.where(mask, row(2 * q), row(2 * q + 1))
        rhs_out[q] = value
        return value / CENTER

    fill_table(table, 12, 48, base, own)
    for side, source, start in ((0, left, 0), (1, right, 60)):
        keep = flags[side] > 0
        unpack_natural(source, by_load, 1.0)

        def ghost(q):
            at = side * GHOST + 2 * q
            value = jnp.where(mask, row(ghosts[at]), row(ghosts[at + 1])) / CENTER
            return jnp.where(keep, value, jnp.zeros_like(value))

        fill_table(table, start, 12, base, ghost)

    def step(g, _):
        products = operator_group(table, base, 12, g, index_ref, ROWS, high_ref, low_ref)
        for j in range(2):
            q = 2 * g + j
            direction = table[12 + q]
            update_step(
                q, products[j], rhs_out[q], direction, direction, FACTORS[0], (r_out, d_out, x_out)
            )
        return 0

    lax.fori_loop(0, 24, step, 0, unroll=2)
    gather_sends(d_out, send_ref, to_left, to_right)


def fill_one(flags, vector, left, right, table):
    base = 72
    fill_table(table, 12, 48, base, lambda q: vector[q])
    for side, source, start in ((0, left, 0), (1, right, 60)):
        keep = flags[side] > 0
        fill_table(
            table, start, 12, base,
            lambda q: jnp.where(keep, source[q], jnp.zeros((8, 128), f32)),
        )


def one_kernel(
    flags, index_ref, send_ref, vector, left, right, residual, solution, high_ref, low_ref,
    r_out, d_out, x_out, to_left, to_right, table, *, factors,
):
    fill_one(flags, vector, left, right, table)

    def step(g, _):
        products = operator_group(table, 72, 12, g, index_ref, ROWS, high_ref, low_ref)
        for j in range(2):
            q = 2 * g + j
            start = vector[q] if solution is None else solution[q]
            update_step(
                q, products[j], residual[q], vector[q], start, factors, (r_out, d_out, x_out)
            )
        return 0

    lax.fori_loop(0, 24, step, 0, unroll=2)
    gather_sends(d_out, send_ref, to_left, to_right)


def restrict_one_kernel(
    flags, index_ref, agg_ref, vector, left, right, residual, high_ref, low_ref, prol_h, prol_l,
    out, table, sums,
):
    fill_one(flags, vector, left, right, table)
    zero_sums(sums, ROWS)

    def step(g, _):
        products = operator_group(table, 72, 12, g, index_ref, ROWS, high_ref, low_ref)
        finals = [residual[2 * g + j] - products[j] for j in range(2)]
        restrict_group(finals[0], finals[1], g, agg_ref, prol_h, prol_l, sums)
        return 0

    lax.fori_loop(0, 24, step, 0, unroll=2)
    pack_sums(sums, out, ROWS)


def last_one_kernel(
    flags, index_ref, vector, left, right, residual, solution, high_ref, low_ref,
    out, table, by_load,
):
    fill_one(flags, vector, left, right, table)
    factors = FACTORS[1]

    def step(g, _):
        products = operator_group(table, 72, 12, g, index_ref, ROWS, high_ref, low_ref)
        for j in range(2):
            q = 2 * g + j
            direction = factors[0] * vector[q] + factors[1] * (residual[q] - products[j])
            value = solution[q] + direction
            by_load[pl.ds(pl.multiple_of(16 * q, 16), 8), :] = value
            by_load[pl.ds(pl.multiple_of(16 * q + 8, 8), 8), :] = swap(value)
        return 0

    lax.fori_loop(0, 24, step, 0, unroll=2)
    mask = low_lanes((ROWS, 128))
    for t in range(4):
        even = by_load[pl.ds(2 * t, ROWS, stride=8), :]
        odd = by_load[pl.ds(2 * t + 1, ROWS, stride=8), :]
        out[:, 128 * t : 128 * t + 128] = jnp.where(mask, even, swap(odd))


def fill_two(flags, vector, left, right, table, scale):
    base = 144
    for side, source, start in ((0, left, 0), (None, vector, 48), (1, right, 96)):
        if side is None:
            read = lambda q: source[q] / CENTER if scale else source[q]
        else:
            keep = flags[side] > 0

            def read(q):
                value = source[q] / CENTER if scale else source[q]
                return jnp.where(keep, value, jnp.zeros_like(value))

        fill_table(table, start, 48, base, read)


def two_kernel(
    flags, index_ref, vector, left, right, residual, solution, high_ref, low_ref,
    r_out, d_out, x_out, table, *, factors, scale,
):
    fill_two(flags, vector, left, right, table, scale)

    def step(g, _):
        products = operator_group(table, 144, 48, g, index_ref, ROWS, high_ref, low_ref)
        for j in range(2):
            q = 2 * g + j
            direction = table[48 + q]
            start = direction if solution is None else solution[q]
            update_step(
                q, products[j], residual[q], direction, start, factors, (r_out, d_out, x_out)
            )
        return 0

    lax.fori_loop(0, 24, step, 0, unroll=2)


def restrict_two_kernel(
    flags, index_ref, agg_ref, vector, left, right, residual, high_ref, low_ref, prol_h, prol_l,
    out, table, sums,
):
    fill_two(flags, vector, left, right, table, False)
    zero_sums(sums, COARSE)

    def step(g, _):
        products = operator_group(table, 144, 48, g, index_ref, ROWS, high_ref, low_ref)
        finals = [residual[2 * g + j] - products[j] for j in range(2)]
        restrict_group(finals[0], finals[1], g, agg_ref, prol_h, prol_l, sums)
        return 0

    lax.fori_loop(0, 12, step, 0, unroll=2)
    pack_sums(sums, out, COARSE)


def coarse_kernel(
    index_ref, agg_ref, rhs, smooth, high_ref, low_ref, own_h, own_l, other_h, other_l,
    coarse_out, corrected_out, table, residual, direction,
):
    base = COARSE // 2

    def start(q, _):
        value = rhs[q]
        residual[q] = value
        direction[q] = value / CENTER
        coarse_out[q] = value / CENTER
        return 0

    lax.fori_loop(0, base, start, 0, unroll=4)
    for factors in FACTORS:
        fill_table(table, 0, base, base, lambda q: direction[q])

        def step(g, _):
            products = operator_group(table, base, 0, g, index_ref, COARSE, high_ref, low_ref)
            for j in range(2):
                q = 2 * g + j
                now = residual[q] - products[j]
                residual[q] = now
                turned = factors[0] * direction[q] + factors[1] * now
                direction[q] = turned
                coarse_out[q] = coarse_out[q] + turned
            return 0

        lax.fori_loop(0, COARSE // 4, step, 0, unroll=2)
    fill_table(table, 0, base, base, lambda q: coarse_out[q])
    for start_g, high_p, low_p in ((0, own_h, own_l), (12, other_h, other_l)):

        def lift(g, _):
            products = prolong_group(table, base, g, agg_ref, high_p, low_p, 4 * start_g)
            for j in range(2):
                q = 2 * (start_g + g) + j
                corrected_out[q] = smooth[q] + products[j]
            return 0

        lax.fori_loop(0, 12, lift, 0, unroll=2)


def lift_kernel(
    flags, index_ref, agg_ref, send_ref, vector, left, right, residual, solution, high_ref, low_ref,
    smooth, prol_h, prol_l, corrected_out, to_left, to_right, table, lifted,
):
    fill_two(flags, vector, left, right, table, False)
    factors = FACTORS[1]

    def step(g, _):
        products = operator_group(table, 144, 48, g, index_ref, ROWS, high_ref, low_ref)
        for j in range(2):
            q = 2 * g + j
            direction = factors[0] * table[48 + q] + factors[1] * (residual[q] - products[j])
            value = solution[q] + direction
            lifted[q] = value
            lifted[48 + q] = swap(value)
        return 0

    lax.fori_loop(0, 24, step, 0, unroll=2)

    def lift(g, _):
        products = prolong_group(lifted, 48, g, agg_ref, prol_h, prol_l, 0)
        for j in range(2):
            q = 2 * g + j
            corrected_out[q] = smooth[q] + products[j]
        return 0

    lax.fori_loop(0, 24, lift, 0, unroll=2)
    gather_sends(corrected_out, send_ref, to_left, to_right)


def packed(pairs):
    return jax.ShapeDtypeStruct((pairs, 8, 128), f32)


def call(kernel, scalars, arrays, outs, scratch, weight):
    return pl.pallas_call(
        kernel,
        out_shape=outs,
        in_specs=[SM] * len(scalars) + [VM] * len(arrays),
        out_specs=jax.tree.map(lambda _: VM, outs),
        scratch_shapes=[pltpu.VMEM(shape, f32) for shape in scratch],
        compiler_params=pltpu.CompilerParams(vmem_limit_bytes=24 * 1024 * 1024),
        cost_estimate=pl.CostEstimate(
            flops=weight * 10**9, bytes_accessed=8 * 2**20, transcendentals=0
        ),
    )(*scalars, *arrays)


def drop(kernel, position, **options):
    def run(*refs):
        return kernel(*refs[:position], None, *refs[position:], **options)

    return run


def exchange(value, pairs):
    return lax.ppermute(value, AXES, pairs)


def high_half(rows):
    return 1 - (rows & 1), rows >> 1


def body(
    right_side, ghost_rows, cols_one, diag_one, offd_one, prol_one, agg_one, cols_two, diag_two,
    offd_two, prol_two, agg_two, cols_three, diag_three, offd_three,
):
    blocks = lax.axis_size("grp") * lax.axis_size("dev")
    block = lax.axis_index("grp") * lax.axis_size("dev") + lax.axis_index("dev")
    half = block % 2
    pair = block // 2

    def shift(value, steps):
        return exchange(value, [(s, (s + steps) % blocks) for s in range(blocks)])

    def flip(value, mask):
        return exchange(value, [(s, s ^ mask) for s in range(blocks)])

    left_raw = shift(right_side, 1)
    right_raw = shift(right_side, -1)
    lists = jnp.concatenate([shift(ghost_rows[1], 1), shift(ghost_rows[0], -1)])

    flags_one = jnp.stack([block > 0, block < blocks - 1]).astype(jnp.int32)
    flags_two = jnp.stack([pair > 0, pair < blocks // 2 - 1]).astype(jnp.int32)

    def slots(first, second, base):
        return jnp.concatenate(
            [(1 - (first & 1)) * base + (first >> 1), (second & 1) * base + (second >> 1)]
        )

    def low_slot(rows, base):
        return (rows & 1) * base + (rows >> 1)

    def local_row(rows):
        return (rows + half * HALF) % ROWS

    index_one = slots(cols_one[:, 0], cols_one[:, 1], 72)
    cols_pair = jnp.concatenate([cols_two, flip(cols_two, 1)], 0)
    cols_pair = (cols_pair // ROWS) * ROWS + local_row(cols_pair % ROWS)
    index_two = slots(cols_pair[:, 0], cols_pair[:, 1], 144)
    index_three = slots(cols_three[:, 0], cols_three[:, 1], COARSE // 2)
    agg_pair = low_slot(jnp.concatenate([agg_two, flip(agg_two, 1)]), COARSE // 2)
    agg_local = local_row(agg_one)
    lift_index = low_slot(agg_local, 48)

    def tiles(flat):
        return flat.reshape(flat.shape[:-1] + (32, 128))

    one_w = prepare_operator([(tiles(diag_one), tiles(offd_one))])
    one_p = prepare_transfer(tiles(prol_one))
    two_w = prepare_operator(
        [
            (tiles(diag_two), tiles(offd_two)),
            (tiles(flip(diag_two, 1)), tiles(flip(offd_two, 1))),
        ]
    )
    two_p = prepare_transfer(tiles(prol_two))
    two_p_other = prepare_transfer(tiles(flip(prol_two, 1)))
    three_w = prepare_operator([(tiles(diag_three), tiles(offd_three))])

    v48, v12 = packed(48), packed(12)
    table_one, table_two = (144, 8, 128), (288, 8, 128)
    by_load = (ROWS * 8, 128)

    rhs, r, d, x, to_left, to_right = call(
        first_one_kernel,
        (flags_one, ghost_rows.reshape(-1), index_one, lists),
        (right_side, left_raw, right_raw, *one_w),
        (v48, v48, v48, v48, v12, v12),
        (table_one, by_load),
        2,
    )

    def one_turn(d, r, x, to_left, to_right, factors):
        from_left, from_right = shift(to_right, 1), shift(to_left, -1)
        return call(
            functools.partial(one_kernel, factors=factors),
            (flags_one, index_one, lists),
            (d, from_left, from_right, r, x, *one_w),
            (v48, v48, v48, v12, v12),
            (table_one,),
            2,
        )

    r, d, smooth_one, to_left, to_right = one_turn(d, r, x, to_left, to_right, FACTORS[1])
    part = call(
        restrict_one_kernel,
        (flags_one, index_one, agg_local),
        (d, shift(to_right, 1), shift(to_left, -1), r, *one_w, *one_p),
        v48,
        (table_one, (ROWS, 8, 128)),
        3,
    )
    other = flip(part, 1)
    rhs_two = part + jnp.concatenate([other[24:], other[:24]], 0)

    def two_turn(d, r, x, factors, scale=False):
        from_left, from_right = shift(d, 2), shift(d, -2)
        kernel = functools.partial(two_kernel, factors=factors, scale=scale)
        arrays = [d, from_left, from_right, r, *two_w]
        if x is None:
            kernel = drop(two_kernel, 6, factors=factors, scale=scale)
        else:
            arrays.insert(4, x)
        return call(
            kernel, (flags_two, index_two), arrays, (v48, v48, v48), (table_two,), 2
        )

    r, d, x = two_turn(rhs_two, rhs_two, None, FACTORS[0], True)
    r, d, smooth_two = two_turn(d, r, x, FACTORS[1])
    coarse_rhs = call(
        restrict_two_kernel,
        (flags_two, index_two, agg_pair_own(agg_two)),
        (d, shift(d, 2), shift(d, -2), r, *two_w, *two_p),
        packed(COARSE // 2),
        (table_two, (COARSE, 8, 128)),
        2,
    )
    for masks in reduce_phases(blocks):
        others = [flip(coarse_rhs, m) for m in masks]
        if len(masks) == 1:
            coarse_rhs = coarse_rhs + others[0]
        else:
            coarse_rhs = (coarse_rhs + others[0]) + (others[1] + others[2])

    coarse, corrected_two = call(
        coarse_kernel,
        (index_three, agg_pair),
        (coarse_rhs, smooth_two, *three_w, *two_p, *two_p_other),
        (packed(COARSE // 2), v48),
        ((COARSE, 8, 128), (COARSE // 2, 8, 128), (COARSE // 2, 8, 128)),
        4,
    )

    r, d, x = two_turn(corrected_two, rhs_two, corrected_two, None)
    r, d, x = two_turn(d, r, x, FACTORS[0])
    corrected_one, to_left, to_right = call(
        lift_kernel,
        (flags_two, index_two, lift_index, lists),
        (d, shift(d, 2), shift(d, -2), r, x, *two_w, smooth_one, *one_p),
        (v48, v12, v12),
        (table_two, (ROWS, 8, 128)),
        3,
    )

    r, d, x, to_left, to_right = one_turn(
        corrected_one, rhs, corrected_one, to_left, to_right, None
    )
    r, d, x, to_left, to_right = one_turn(d, r, x, to_left, to_right, FACTORS[0])
    solution = call(
        last_one_kernel,
        (flags_one, index_one),
        (d, shift(to_right, 1), shift(to_left, -1), r, x, *one_w),
        jax.ShapeDtypeStruct((ROWS, LOADS * TILE), f32),
        (table_one, by_load),
        2,
    )
    coarse_solution = (
        coarse.reshape(COARSE // 2, LOADS, 2, TILE).transpose(0, 2, 1, 3).reshape(COARSE, -1)
    )
    return solution, coarse_solution


def agg_pair_own(agg_two):
    return agg_two


def reduce_phases(blocks):
    if blocks == 256:
        return ((32,), (1, 2, 3), (4,), (8, 16, 24), (64, 128, 192))
    return tuple((1 << bit,) for bit in range(blocks.bit_length() - 1))


def solution(mesh):
    rows = P(AXES, None)
    return jax.shard_map(
        body,
        mesh=mesh,
        in_specs=(
            rows, rows, rows, rows, P(AXES, None, None), rows, P(AXES), rows, rows,
            P(AXES, None, None), rows, P(AXES), P(), P(), P(),
        ),
        out_specs=(rows, P()),
        check_vma=False,
    )
```

```python
import functools

import jax
import jax.numpy as jnp
from jax import lax
from jax.experimental import pallas as pl
from jax.experimental.pallas import tpu as pltpu
from jax.sharding import PartitionSpec as P

TILE = 64
LOADS = 8
ROWS = 96
HALF = 48
COARSE = 32
GHOST = 24
AXES = ("grp", "dev")
VMEM_LIMIT = 8 * 2**20

CENTER = 5.0
RADIUS = 4.0
SIGMA = 1.25

bf16 = jnp.bfloat16
f32 = jnp.float32
VM = pl.BlockSpec(memory_space=pltpu.VMEM)
SM = pl.BlockSpec(memory_space=pltpu.SMEM)


def chebyshev_factors(count):
    rho = 1.0 / SIGMA
    factors = []
    for _ in range(count):
        rho_next = 1.0 / (2.0 * SIGMA - rho)
        factors.append((rho_next * rho, 2.0 * rho_next / RADIUS))
        rho = rho_next
    return factors


FACTORS = chebyshev_factors(7)


def low_lanes(shape):
    return lax.broadcasted_iota(jnp.int32, shape, len(shape) - 1) < TILE


def swap(value):
    return pltpu.roll(value, TILE, value.ndim - 1)


def each(count, step):
    for at in range(count):
        step(at)


def split(value):
    high = value.astype(bf16)
    return high, (value - high.astype(f32)).astype(bf16)


def dot_nt(a, b):
    return lax.dot_general(a, b, (((1,), (1,)), ((), ())), preferred_element_type=f32)


def dot_nn(a, b):
    return lax.dot_general(a, b, (((1,), (0,)), ((), ())), preferred_element_type=f32)


def fill_table(table, start, count, base, read):
    for q in range(count):
        value = read(q)
        table[start + q] = value
        table[base + start + q] = swap(value)


def block_products(left, high_w, low_w):
    high, low = split(left)
    both = dot_nn(jnp.concatenate([high, low], 0), high_w)
    rest = dot_nn(high, low_w)
    mask = low_lanes((8, 128))

    def block(i):
        lanes = slice((i // 2) * 128, (i // 2) * 128 + 128)
        return (
            both[8 * i : 8 * i + 8, lanes]
            + both[32 + 8 * i : 40 + 8 * i, lanes]
            + rest[8 * i : 8 * i + 8, lanes]
        )

    return [jnp.where(mask, block(2 * j), block(2 * j + 1)) for j in range(2)]


def operator_group(table, base, own, g, index_ref, count, high_ref, low_ref):
    mask = low_lanes((8, 128))
    rows = []
    for i in range(4):
        mine = table[(i & 1) * base + own + 2 * g + (i >> 1)]
        first = table[index_ref[4 * g + i]]
        second = table[index_ref[count + 4 * g + i]]
        rows.append(jnp.concatenate([jnp.where(mask, mine, first), second], 1))
    left = jnp.concatenate(rows, 0)[:, : 3 * TILE]
    return block_products(left, high_ref[g], low_ref[g])


def prolong_group(table, base, g, index_ref, high_ref, low_ref, row_start):
    rows = [table[index_ref[row_start + 4 * g + i]] for i in range(4)]
    left = jnp.concatenate(rows, 0)[:, :TILE]
    return block_products(left, high_ref[g], low_ref[g])


def restrict_group(pair0, pair1, g, agg_ref, high_ref, low_ref, sums):
    mask = low_lanes((8, 128))
    zero = jnp.zeros((8, 128), f32)
    rows = [
        jnp.concatenate([jnp.where(mask, pair0, zero), zero], 1),
        jnp.concatenate([jnp.where(mask, zero, pair0), zero], 1),
        jnp.concatenate([zero, jnp.where(mask, pair1, zero)], 1),
        jnp.concatenate([zero, jnp.where(mask, zero, pair1)], 1),
    ]
    high, low = split(jnp.concatenate(rows, 0))
    both = dot_nt(jnp.concatenate([high, low], 0), high_ref[g])
    terms = both[:32] + both[32:] + dot_nt(high, low_ref[g])
    for i in range(4):
        row = agg_ref[4 * g + i]
        sums[row, :, :TILE] = sums[row, :, :TILE] + terms[8 * i : 8 * i + 8]


def zero_sums(sums, count):
    def step(q):
        sums[q] = jnp.zeros((8, 128), f32)

    each(count, step)


def pack_sums(sums, out, count):
    def step(q):
        out[q] = sums[2 * q] + swap(sums[2 * q + 1])

    each(count // 2, step)


def gather_sends(vector, send_ref, to_left, to_right):
    mask = low_lanes((8, 128))

    def half(row, odd):
        value = vector[row >> 1]
        return jnp.where((row & 1) == odd, value, swap(value))

    def step(q):
        for side, out in ((0, to_left), (1, to_right)):
            at = side * GHOST + 2 * q
            out[q] = jnp.where(mask, half(send_ref[at], 0), half(send_ref[at + 1], 1))

    each(GHOST // 2, step)


def prepare_operator_kernel(diag_ref, offd_ref, high_ref, low_ref, token, stage_a, stage_b):
    token[0] = 0
    mask = low_lanes((32, 128))
    for i in range(8):
        diag, first, second = diag_ref[i], offd_ref[i, 0], offd_ref[i, 1]
        even, odd = pl.ds(64 * i, 32, stride=2), pl.ds(64 * i + 1, 32, stride=2)
        stage_a[even, :] = jnp.where(mask, diag, swap(first))
        stage_a[odd, :] = jnp.where(mask, swap(diag), first)
        stage_b[even, :] = second
        stage_b[odd, :] = swap(second)
    for j in range(2):
        rows = slice(256 * j, 256 * j + 256)
        for stage, count, at in ((stage_a, 128, 0), (stage_b, 64, 128)):
            high, low = split(stage[rows, :].T[:count])
            high_ref[j, at : at + count, :] = high
            low_ref[j, at : at + count, :] = low


def prepare_operator(diag, offd):
    rows = diag.shape[0]
    out = jax.ShapeDtypeStruct((rows // 4, 3 * TILE, 256), bf16)
    out_spec = pl.BlockSpec((2, 3 * TILE, 256), lambda g: (g, 0, 0))
    return pl.pallas_call(
        prepare_operator_kernel,
        out_shape=(out, out, jax.ShapeDtypeStruct((1,), jnp.int32)),
        grid=(rows // 8,),
        in_specs=[
            pl.BlockSpec((8, 32, 128), lambda g: (g, 0, 0)),
            pl.BlockSpec((8, 2, 32, 128), lambda g: (g, 0, 0, 0)),
        ],
        out_specs=(out_spec, out_spec, SM),
        scratch_shapes=[pltpu.VMEM((512, 128), f32), pltpu.VMEM((512, 128), f32)],
        compiler_params=pltpu.CompilerParams(vmem_limit_bytes=VMEM_LIMIT),
        cost_estimate=pl.CostEstimate(
            flops=rows * 5 * 10**7, bytes_accessed=rows * 114688, transcendentals=0
        ),
    )(diag, offd)


def prepare_transfer_kernel(prol_ref, high_ref, low_ref, stage):
    for i in range(8):
        prol = prol_ref[i]
        stage[pl.ds(64 * i, 32, stride=2), :] = prol
        stage[pl.ds(64 * i + 1, 32, stride=2), :] = swap(prol)
    for j in range(2):
        high, low = split(stage[256 * j : 256 * j + 256, :].T[:TILE])
        high_ref[j] = high
        low_ref[j] = low


def prepare_transfer(prol):
    rows = prol.shape[0]
    out = jax.ShapeDtypeStruct((rows // 4, TILE, 256), bf16)
    out_spec = pl.BlockSpec((2, TILE, 256), lambda g: (g, 0, 0))
    return pl.pallas_call(
        prepare_transfer_kernel,
        out_shape=(out, out),
        grid=(rows // 8,),
        in_specs=[pl.BlockSpec((8, 32, 128), lambda g: (g, 0, 0))],
        out_specs=(out_spec, out_spec),
        scratch_shapes=[pltpu.VMEM((512, 128), f32)],
        compiler_params=pltpu.CompilerParams(vmem_limit_bytes=VMEM_LIMIT),
        cost_estimate=pl.CostEstimate(
            flops=rows * 2 * 10**7, bytes_accessed=rows * 32768, transcendentals=0
        ),
    )(prol)


def unpack_natural(source, rows_by_load, scale):
    mask = low_lanes((ROWS, 128))
    for t in range(4):
        value = source[:, 128 * t : 128 * t + 128] * scale
        other = swap(value)
        rows_by_load[pl.ds(2 * t, ROWS, stride=8), :] = jnp.where(mask, value, other)
        rows_by_load[pl.ds(2 * t + 1, ROWS, stride=8), :] = jnp.where(mask, other, value)


def update_step(q, product, residual_in, direction_in, solution_in, factors, outs):
    residual = residual_in - product
    if factors is None:
        direction = residual / CENTER
    else:
        direction = factors[0] * direction_in + factors[1] * residual
    outs[0][q] = residual
    outs[1][q] = direction
    outs[2][q] = solution_in + direction


def first_one_kernel(
    flags, ghosts, index_ref, send_ref, mine, left, right, high_ref, low_ref,
    rhs_out, r_out, d_out, x_out, to_left, to_right, table, by_load,
):
    base = 72
    mask = low_lanes((8, 128))

    def row(r):
        return by_load[pl.ds(pl.multiple_of(8 * r, 8), 8), :]

    unpack_natural(mine, by_load, 1.0)

    def own(q):
        value = jnp.where(mask, row(2 * q), row(2 * q + 1))
        rhs_out[q] = value
        return value / CENTER

    fill_table(table, 12, 48, base, own)
    for side, source, start in ((0, left, 0), (1, right, 60)):
        keep = flags[side] > 0
        unpack_natural(source, by_load, 1.0)

        def ghost(q):
            at = side * GHOST + 2 * q
            value = jnp.where(mask, row(ghosts[at]), row(ghosts[at + 1])) / CENTER
            return jnp.where(keep, value, jnp.zeros_like(value))

        fill_table(table, start, 12, base, ghost)

    def step(g):
        products = operator_group(table, base, 12, g, index_ref, ROWS, high_ref, low_ref)
        for j in range(2):
            q = 2 * g + j
            direction = table[12 + q]
            update_step(
                q, products[j], rhs_out[q], direction, direction, FACTORS[0], (r_out, d_out, x_out)
            )

    each(24, step)
    gather_sends(d_out, send_ref, to_left, to_right)


def fill_one(flags, vector, left, right, table):
    base = 72
    fill_table(table, 12, 48, base, lambda q: vector[q])
    for side, source, start in ((0, left, 0), (1, right, 60)):
        keep = flags[side] > 0
        fill_table(
            table, start, 12, base,
            lambda q: jnp.where(keep, source[q], jnp.zeros((8, 128), f32)),
        )


def one_kernel(
    flags, index_ref, send_ref, vector, left, right, residual, solution, high_ref, low_ref,
    r_out, d_out, x_out, to_left, to_right, table, *, factors,
):
    fill_one(flags, vector, left, right, table)

    def step(g):
        products = operator_group(table, 72, 12, g, index_ref, ROWS, high_ref, low_ref)
        for j in range(2):
            q = 2 * g + j
            start = vector[q] if solution is None else solution[q]
            update_step(
                q, products[j], residual[q], vector[q], start, factors, (r_out, d_out, x_out)
            )

    each(24, step)
    gather_sends(d_out, send_ref, to_left, to_right)


def restrict_one_kernel(
    flags, index_ref, agg_ref, vector, left, right, residual, high_ref, low_ref, prol_h, prol_l,
    out, table, sums,
):
    fill_one(flags, vector, left, right, table)
    zero_sums(sums, ROWS)

    def step(g):
        products = operator_group(table, 72, 12, g, index_ref, ROWS, high_ref, low_ref)
        finals = [residual[2 * g + j] - products[j] for j in range(2)]
        restrict_group(finals[0], finals[1], g, agg_ref, prol_h, prol_l, sums)

    each(24, step)
    pack_sums(sums, out, ROWS)


def last_one_kernel(
    flags, index_ref, vector, left, right, residual, solution, high_ref, low_ref,
    out, table, by_load,
):
    fill_one(flags, vector, left, right, table)
    factors = FACTORS[1]

    def step(g):
        products = operator_group(table, 72, 12, g, index_ref, ROWS, high_ref, low_ref)
        for j in range(2):
            q = 2 * g + j
            direction = factors[0] * vector[q] + factors[1] * (residual[q] - products[j])
            value = solution[q] + direction
            by_load[pl.ds(pl.multiple_of(16 * q, 16), 8), :] = value
            by_load[pl.ds(pl.multiple_of(16 * q + 8, 8), 8), :] = swap(value)

    each(24, step)
    mask = low_lanes((ROWS, 128))
    for t in range(4):
        even = by_load[pl.ds(2 * t, ROWS, stride=8), :]
        odd = by_load[pl.ds(2 * t + 1, ROWS, stride=8), :]
        out[:, 128 * t : 128 * t + 128] = jnp.where(mask, even, swap(odd))


def fill_two(flags, vector, left, right, table, scale):
    base = 144
    for side, source, start in ((0, left, 0), (None, vector, 48), (1, right, 96)):
        if side is None:
            read = lambda q: source[q] / CENTER if scale else source[q]
        else:
            keep = flags[side] > 0

            def read(q):
                value = source[q] / CENTER if scale else source[q]
                return jnp.where(keep, value, jnp.zeros_like(value))

        fill_table(table, start, 48, base, read)


def two_kernel(
    flags, index_ref, vector, left, right, residual, solution, high_ref, low_ref,
    r_out, d_out, x_out, table, *, factors, scale,
):
    fill_two(flags, vector, left, right, table, scale)

    def step(g):
        products = operator_group(table, 144, 48, g, index_ref, ROWS, high_ref, low_ref)
        for j in range(2):
            q = 2 * g + j
            direction = table[48 + q]
            start = direction if solution is None else solution[q]
            update_step(
                q, products[j], residual[q], direction, start, factors, (r_out, d_out, x_out)
            )

    each(24, step)


def restrict_two_kernel(
    flags, index_ref, agg_ref, vector, left, right, residual, high_ref, low_ref, prol_h, prol_l,
    out, table, sums,
):
    fill_two(flags, vector, left, right, table, False)
    zero_sums(sums, COARSE)

    def step(g):
        products = operator_group(table, 144, 48, g, index_ref, ROWS, high_ref, low_ref)
        finals = [residual[2 * g + j] - products[j] for j in range(2)]
        restrict_group(finals[0], finals[1], g, agg_ref, prol_h, prol_l, sums)

    each(12, step)
    pack_sums(sums, out, COARSE)


def coarse_kernel(
    index_ref, agg_ref, rhs, smooth, high_ref, low_ref, own_h, own_l, other_h, other_l,
    coarse_out, corrected_out, table, residual, direction,
):
    base = COARSE // 2

    def start(q):
        value = rhs[q]
        residual[q] = value
        direction[q] = value / CENTER
        coarse_out[q] = value / CENTER

    each(base, start)
    for factors in FACTORS:
        fill_table(table, 0, base, base, lambda q: direction[q])

        def step(g):
            products = operator_group(table, base, 0, g, index_ref, COARSE, high_ref, low_ref)
            for j in range(2):
                q = 2 * g + j
                now = residual[q] - products[j]
                residual[q] = now
                turned = factors[0] * direction[q] + factors[1] * now
                direction[q] = turned
                coarse_out[q] = coarse_out[q] + turned

        each(COARSE // 4, step)
    fill_table(table, 0, base, base, lambda q: coarse_out[q])
    for start_g, high_p, low_p in ((0, own_h, own_l), (12, other_h, other_l)):

        def lift(g):
            products = prolong_group(table, base, g, agg_ref, high_p, low_p, 4 * start_g)
            for j in range(2):
                q = 2 * (start_g + g) + j
                corrected_out[q] = smooth[q] + products[j]

        each(12, lift)


def lift_kernel(
    flags, index_ref, agg_ref, send_ref, vector, left, right, residual, solution, smooth, high_ref,
    low_ref, prol_h, prol_l, corrected_out, to_left, to_right, table, lifted,
):
    fill_two(flags, vector, left, right, table, False)
    factors = FACTORS[1]

    def step(g):
        products = operator_group(table, 144, 48, g, index_ref, ROWS, high_ref, low_ref)
        for j in range(2):
            q = 2 * g + j
            direction = factors[0] * table[48 + q] + factors[1] * (residual[q] - products[j])
            value = solution[q] + direction
            lifted[q] = value
            lifted[48 + q] = swap(value)

    each(24, step)

    def lift(g):
        products = prolong_group(lifted, 48, g, agg_ref, prol_h, prol_l, 0)
        for j in range(2):
            q = 2 * g + j
            corrected_out[q] = smooth[q] + products[j]

    each(24, lift)
    gather_sends(corrected_out, send_ref, to_left, to_right)


def packed(pairs):
    return jax.ShapeDtypeStruct((pairs, 8, 128), f32)


class Streamed:
    def __init__(self, sources, buffer, semaphores):
        self.buffer = buffer
        self.copies = []
        start = 0
        for source in sources:
            groups = source.shape[0]
            pieces = 2 if groups >= 12 else 1
            for piece in range(pieces):
                count = groups // pieces
                self.copies.append(
                    (
                        start,
                        pltpu.make_async_copy(
                            source.at[pl.ds(piece * count, count)],
                            buffer.at[pl.ds(start, count)],
                            semaphores.at[len(self.copies)],
                        ),
                    )
                )
                start += count
        self.copies = [c for c in self.copies if c[0] < buffer.shape[0]]

    def __getitem__(self, group):
        while self.copies and self.copies[0][0] <= group:
            self.copies.pop(0)[1].wait()
        return self.buffer[group]


class Parts:
    def __init__(self, refs):
        self.refs = refs

    def __getitem__(self, group):
        for ref in self.refs:
            if group < ref.shape[0]:
                return ref[group]
            group -= ref.shape[0]


def call(kernel, scalars, arrays, weights, outs, scratch, weight, token=False):
    single = not isinstance(outs, tuple)
    if single:
        outs = (outs,)
    parts = [p for w in weights for p in w]
    inputs, results = len(scalars) + len(arrays), len(outs)

    def run(*refs):
        first = refs[:inputs]
        sources = refs[inputs : inputs + len(parts)]
        rest = refs[inputs + len(parts) :]
        results_refs, rest = rest[:results], rest[results:]
        if token:
            rest[0][0] = 0
            rest = rest[1:]
        held, at = [], 0
        for w in weights:
            held.append(Parts(sources[at : at + len(w)]))
            at += len(w)
        kernel(*first, *held, *results_refs, *rest)

    out_shape = tuple(outs) + ((jax.ShapeDtypeStruct((1,), jnp.int32),) if token else ())
    got = pl.pallas_call(
        run,
        out_shape=out_shape,
        in_specs=[SM] * len(scalars) + [VM] * (len(arrays) + len(parts)),
        out_specs=(VM,) * results + ((SM,) if token else ()),
        scratch_shapes=[pltpu.VMEM(shape, f32) for shape in scratch],
        compiler_params=pltpu.CompilerParams(vmem_limit_bytes=VMEM_LIMIT),
        cost_estimate=pl.CostEstimate(
            flops=weight * 10**9, bytes_accessed=8 * 2**20, transcendentals=0
        ),
    )(*scalars, *arrays, *parts)
    return got[0] if single else got


def drop(kernel, position, **options):
    def run(*refs):
        return kernel(*refs[:position], None, *refs[position:], **options)

    return run


def exchange(value, pairs):
    return lax.ppermute(value, AXES, pairs)


def high_half(rows):
    return 1 - (rows & 1), rows >> 1


def body(
    right_side, ghost_rows, cols_one, diag_one, offd_one, prol_one, agg_one, cols_two, diag_two,
    offd_two, prol_two, agg_two, cols_three, diag_three, offd_three,
):
    blocks = lax.axis_size("grp") * lax.axis_size("dev")
    block = lax.axis_index("grp") * lax.axis_size("dev") + lax.axis_index("dev")
    half = block % 2
    pair = block // 2

    def shift(value, steps):
        return exchange(value, [(s, (s + steps) % blocks) for s in range(blocks)])

    def flip(value, mask):
        return exchange(value, [(s, s ^ mask) for s in range(blocks)])

    left_raw = shift(right_side, 1)
    right_raw = shift(right_side, -1)
    lists = jnp.concatenate([shift(ghost_rows[1], 1), shift(ghost_rows[0], -1)])

    flags_one = jnp.stack([block > 0, block < blocks - 1]).astype(jnp.int32)
    flags_two = jnp.stack([pair > 0, pair < blocks // 2 - 1]).astype(jnp.int32)

    def slots(first, second, base):
        return jnp.concatenate(
            [(1 - (first & 1)) * base + (first >> 1), (second & 1) * base + (second >> 1)]
        )

    def low_slot(rows, base):
        return (rows & 1) * base + (rows >> 1)

    def local_row(rows):
        return (rows + half * HALF) % ROWS

    index_one = slots(cols_one[:, 0], cols_one[:, 1], 72)
    cols_pair = jnp.concatenate([cols_two, flip(cols_two, 1)], 0)
    cols_pair = (cols_pair // ROWS) * ROWS + local_row(cols_pair % ROWS)
    index_two = slots(cols_pair[:, 0], cols_pair[:, 1], 144)
    index_three = slots(cols_three[:, 0], cols_three[:, 1], COARSE // 2)
    agg_pair = low_slot(jnp.concatenate([agg_two, flip(agg_two, 1)]), COARSE // 2)
    agg_local = local_row(agg_one)
    lift_index = low_slot(agg_local, 48)

    def tiles(flat):
        return flat.reshape(flat.shape[:-1] + (32, 128))

    def paired(prepared):
        return tuple((w,) for w in prepared[:2])

    one_w = paired(prepare_operator(tiles(diag_one), tiles(offd_one)))
    one_p = paired(prepare_transfer(tiles(prol_one)))
    two_own = prepare_operator(tiles(diag_two), tiles(offd_two))
    two_p = paired(prepare_transfer(tiles(prol_two)))
    three_w = paired(prepare_operator(tiles(diag_three), tiles(offd_three)))
    diag_other = flip(diag_two, 1)

    def offd_part(token, at):
        rows = lax.dynamic_slice_in_dim(offd_two, at + token[0], 24, 0)
        return prepare_operator(tiles(diag_other[at : at + 24]), tiles(flip(rows, 1)))

    v48, v12 = packed(48), packed(12)
    table_one, table_two = (144, 8, 128), (288, 8, 128)
    by_load = (ROWS * 8, 128)

    rhs, r, d, x, to_left, to_right, token = call(
        first_one_kernel,
        (flags_one, ghost_rows.reshape(-1), index_one, lists),
        (right_side, left_raw, right_raw),
        one_w,
        (v48, v48, v48, v48, v12, v12),
        (table_one, by_load),
        2,
        token=True,
    )
    other_parts = [offd_part(token, 0)]

    def one_turn(d, r, x, to_left, to_right, factors, token=False):
        from_left, from_right = shift(to_right, 1), shift(to_left, -1)
        return call(
            functools.partial(one_kernel, factors=factors),
            (flags_one, index_one, lists),
            (d, from_left, from_right, r, x),
            one_w,
            (v48, v48, v48, v12, v12),
            (table_one,),
            2,
            token=token,
        )

    r, d, smooth_one, to_left, to_right, token = one_turn(
        d, r, x, to_left, to_right, FACTORS[1], token=True
    )
    other_parts.append(offd_part(token, 24))
    part = call(
        restrict_one_kernel,
        (flags_one + other_parts[0][2], index_one, agg_local),
        (d, shift(to_right, 1), shift(to_left, -1), r),
        (*one_w, *one_p),
        v48,
        (table_one, (ROWS, 8, 128)),
        3,
    )
    two_w = tuple((two_own[k], *[p[k] for p in other_parts]) for k in range(2))
    other = flip(part, 1)
    rhs_two = part + jnp.concatenate([other[24:], other[:24]], 0)

    def two_turn(d, r, x, factors, scale=False, token=False):
        from_left, from_right = shift(d, 2), shift(d, -2)
        kernel = functools.partial(two_kernel, factors=factors, scale=scale)
        arrays = [d, from_left, from_right, r]
        if x is None:
            kernel = drop(two_kernel, 6, factors=factors, scale=scale)
        else:
            arrays.append(x)
        return call(
            kernel,
            (flags_two, index_two),
            arrays,
            two_w,
            (v48, v48, v48),
            (table_two,),
            2,
            token=token,
        )

    r, d, x, token = two_turn(rhs_two, rhs_two, None, FACTORS[0], scale=True, token=True)
    two_p_other = paired(
        prepare_transfer(tiles(flip(lax.dynamic_slice_in_dim(prol_two, token[0], HALF, 0), 1)))
    )
    r, d, smooth_two = two_turn(d, r, x, FACTORS[1])
    coarse_rhs = call(
        restrict_two_kernel,
        (flags_two, index_two, agg_two),
        (d, shift(d, 2), shift(d, -2), r),
        (*[w[:1] for w in two_w], *two_p),
        packed(COARSE // 2),
        (table_two, (COARSE, 8, 128)),
        2,
    )
    for masks in reduce_phases(blocks):
        others = [flip(coarse_rhs, m) for m in masks]
        if len(masks) == 1:
            coarse_rhs = coarse_rhs + others[0]
        else:
            coarse_rhs = (coarse_rhs + others[0]) + (others[1] + others[2])

    coarse, corrected_two = call(
        coarse_kernel,
        (index_three, agg_pair),
        (coarse_rhs, smooth_two),
        (*three_w, *two_p, *two_p_other),
        (packed(COARSE // 2), v48),
        ((COARSE, 8, 128), (COARSE // 2, 8, 128), (COARSE // 2, 8, 128)),
        4,
    )

    r, d, x = two_turn(corrected_two, rhs_two, corrected_two, None)
    r, d, x = two_turn(d, r, x, FACTORS[0])
    corrected_one, to_left, to_right = call(
        lift_kernel,
        (flags_two, index_two, lift_index, lists),
        (d, shift(d, 2), shift(d, -2), r, x, smooth_one),
        (*two_w, *one_p),
        (v48, v12, v12),
        (table_two, (ROWS, 8, 128)),
        3,
    )

    r, d, x, to_left, to_right = one_turn(
        corrected_one, rhs, corrected_one, to_left, to_right, None
    )
    r, d, x, to_left, to_right = one_turn(d, r, x, to_left, to_right, FACTORS[0])
    solution = call(
        last_one_kernel,
        (flags_one, index_one),
        (d, shift(to_right, 1), shift(to_left, -1), r, x),
        one_w,
        jax.ShapeDtypeStruct((ROWS, LOADS * TILE), f32),
        (table_one, by_load),
        2,
    )
    coarse_solution = (
        coarse.reshape(COARSE // 2, LOADS, 2, TILE).transpose(0, 2, 1, 3).reshape(COARSE, -1)
    )
    return solution, coarse_solution


def reduce_phases(blocks):
    if blocks == 256:
        return ((32,), (1, 2, 3), (4,), (8, 16, 24), (64, 128, 192))
    return tuple((1 << bit,) for bit in range(blocks.bit_length() - 1))


def solution(mesh):
    rows = P(AXES, None)
    return jax.shard_map(
        body,
        mesh=mesh,
        in_specs=(
            rows, rows, rows, rows, P(AXES, None, None), rows, P(AXES), rows, rows,
            P(AXES, None, None), rows, P(AXES), P(), P(), P(),
        ),
        out_specs=(rows, P()),
        check_vma=False,
    )
```

```python
import functools

import jax
import jax.numpy as jnp
from jax import lax
from jax.experimental import pallas as pl
from jax.experimental.pallas import tpu as pltpu
from jax.sharding import PartitionSpec as P

TILE = 64
LOADS = 8
ROWS = 96
HALF = 48
COARSE = 32
GHOST = 24
AXES = ("grp", "dev")
VMEM_LIMIT = 8 * 2**20

CENTER = 5.0
RADIUS = 4.0
SIGMA = 1.25

bf16 = jnp.bfloat16
f32 = jnp.float32
VM = pl.BlockSpec(memory_space=pltpu.VMEM)
SM = pl.BlockSpec(memory_space=pltpu.SMEM)


def chebyshev_factors(count):
    rho = 1.0 / SIGMA
    factors = []
    for _ in range(count):
        rho_next = 1.0 / (2.0 * SIGMA - rho)
        factors.append((rho_next * rho, 2.0 * rho_next / RADIUS))
        rho = rho_next
    return factors


FACTORS = chebyshev_factors(7)


def low_lanes(shape):
    return lax.broadcasted_iota(jnp.int32, shape, len(shape) - 1) < TILE


def swap(value):
    return pltpu.roll(value, TILE, value.ndim - 1)


def each(count, step):
    for at in range(count):
        step(at)


def split(value):
    high = value.astype(bf16)
    return high, (value - high.astype(f32)).astype(bf16)


def dot_nt(a, b):
    return lax.dot_general(a, b, (((1,), (1,)), ((), ())), preferred_element_type=f32)


def dot_nn(a, b):
    return lax.dot_general(a, b, (((1,), (0,)), ((), ())), preferred_element_type=f32)


def fill_table(table, start, count, base, read):
    for q in range(count):
        value = read(q)
        table[start + q] = value
        table[base + start + q] = swap(value)


def block_products(left, high_w, low_w):
    high, low = split(left)
    both = dot_nn(jnp.concatenate([high, low], 0), high_w)
    rest = dot_nn(high, low_w)
    mask = low_lanes((8, 128))

    def block(i):
        lanes = slice((i // 2) * 128, (i // 2) * 128 + 128)
        return (
            both[8 * i : 8 * i + 8, lanes]
            + both[32 + 8 * i : 40 + 8 * i, lanes]
            + rest[8 * i : 8 * i + 8, lanes]
        )

    return [jnp.where(mask, block(2 * j), block(2 * j + 1)) for j in range(2)]


def operator_group(table, base, own, g, index_ref, count, high_ref, low_ref):
    mask = low_lanes((8, 128))
    rows = []
    for i in range(4):
        mine = table[(i & 1) * base + own + 2 * g + (i >> 1)]
        first = table[index_ref[4 * g + i]]
        second = table[index_ref[count + 4 * g + i]]
        rows.append(jnp.concatenate([jnp.where(mask, mine, first), second], 1))
    left = jnp.concatenate(rows, 0)[:, : 3 * TILE]
    return block_products(left, high_ref[g], low_ref[g])


def prolong_group(table, base, g, index_ref, high_ref, low_ref, row_start):
    rows = [table[index_ref[row_start + 4 * g + i]] for i in range(4)]
    left = jnp.concatenate(rows, 0)[:, :TILE]
    return block_products(left, high_ref[g], low_ref[g])


def restrict_group(pair0, pair1, g, agg_ref, high_ref, low_ref, sums):
    mask = low_lanes((8, 128))
    zero = jnp.zeros((8, 128), f32)
    rows = [
        jnp.concatenate([jnp.where(mask, pair0, zero), zero], 1),
        jnp.concatenate([jnp.where(mask, zero, pair0), zero], 1),
        jnp.concatenate([zero, jnp.where(mask, pair1, zero)], 1),
        jnp.concatenate([zero, jnp.where(mask, zero, pair1)], 1),
    ]
    high, low = split(jnp.concatenate(rows, 0))
    both = dot_nt(jnp.concatenate([high, low], 0), high_ref[g])
    terms = both[:32] + both[32:] + dot_nt(high, low_ref[g])
    for i in range(4):
        row = agg_ref[4 * g + i]
        sums[row, :, :TILE] = sums[row, :, :TILE] + terms[8 * i : 8 * i + 8]


def zero_sums(sums, count):
    def step(q):
        sums[q] = jnp.zeros((8, 128), f32)

    each(count, step)


def pack_sums(sums, out, count):
    def step(q):
        out[q] = sums[2 * q] + swap(sums[2 * q + 1])

    each(count // 2, step)


def gather_sends(vector, send_ref, to_left, to_right):
    mask = low_lanes((8, 128))

    def half(row, odd):
        value = vector[row >> 1]
        return jnp.where((row & 1) == odd, value, swap(value))

    def step(q):
        for side, out in ((0, to_left), (1, to_right)):
            at = side * GHOST + 2 * q
            out[q] = jnp.where(mask, half(send_ref[at], 0), half(send_ref[at + 1], 1))

    each(GHOST // 2, step)


PITCH = 72


def prepare_operator_kernel(diag_ref, offd_ref, high_ref, low_ref, token, stage_a, stage_b):
    token[0] = 0
    mask = low_lanes((8, 128))
    for s in range(32):
        lanes = slice(128 * s, 128 * s + 128)
        diag, first, second = diag_ref[:, lanes], offd_ref[:, 0, lanes], offd_ref[:, 1, lanes]
        even, odd = pl.ds(2 * s, 8, stride=PITCH), pl.ds(2 * s + 1, 8, stride=PITCH)
        stage_a[even, :] = jnp.where(mask, diag, swap(first))
        stage_a[odd, :] = jnp.where(mask, swap(diag), first)
        stage_b[even, :] = second
        stage_b[odd, :] = swap(second)
    store_turned(((stage_a, 128, 0), (stage_b, 64, 128)), high_ref, low_ref)


def store_turned(stages, high_ref, low_ref):
    for j in range(2):
        for stage, count, at in stages:
            rows = [stage[pl.ds(PITCH * (4 * j + i), TILE), :] for i in range(4)]
            high, low = split(jnp.concatenate(rows, 0).T[:count])
            high_ref[j, at : at + count, :] = high
            low_ref[j, at : at + count, :] = low


def prepare_transfer_kernel(prol_ref, high_ref, low_ref, token, stage):
    token[0] = 0
    for s in range(32):
        prol = prol_ref[:, 128 * s : 128 * s + 128]
        stage[pl.ds(2 * s, 8, stride=PITCH), :] = prol
        stage[pl.ds(2 * s + 1, 8, stride=PITCH), :] = swap(prol)
    store_turned(((stage, 64, 0),), high_ref, low_ref)


def prepare(tile_arrays, rows, start=0, after=()):
    operator = len(tile_arrays) == 2
    depth = 3 * TILE if operator else TILE
    out = jax.ShapeDtypeStruct((rows // 4, depth, 256), bf16)
    out_spec = pl.BlockSpec((2, depth, 256), lambda g: (g, 0, 0))
    first = start // 8
    specs = [pl.BlockSpec((8, 4096), lambda g: (g + first, 0))]
    if operator:
        specs.append(pl.BlockSpec((8, 2, 4096), lambda g: (g, 0, 0)))
    kernel = prepare_operator_kernel if operator else prepare_transfer_kernel

    def run(*refs):
        return kernel(*refs[len(after) :])

    return pl.pallas_call(
        run,
        out_shape=(out, out, jax.ShapeDtypeStruct((1,), jnp.int32)),
        grid=(rows // 8,),
        in_specs=[order_spec(a) for a in after] + specs,
        out_specs=(out_spec, out_spec, SM),
        scratch_shapes=[pltpu.VMEM((8 * PITCH, 128), f32)] * (2 if operator else 1),
        compiler_params=pltpu.CompilerParams(vmem_limit_bytes=VMEM_LIMIT),
        cost_estimate=pl.CostEstimate(
            flops=rows * (8 if operator else 4) * 10**7,
            bytes_accessed=rows * (98304 if operator else 32768),
            transcendentals=0,
        ),
    )(*after, *tile_arrays)


def combine_kernel(mine, other, out):
    for q in range(HALF):
        out[q] = mine[q] + other[(q + 24) % 48]


def combine(mine, other):
    return pl.pallas_call(
        combine_kernel,
        out_shape=packed(48),
        in_specs=[VM, VM],
        out_specs=VM,
        compiler_params=pltpu.CompilerParams(vmem_limit_bytes=VMEM_LIMIT),
    )(mine, other)


def unpack_natural(source, rows_by_load, scale):
    mask = low_lanes((ROWS, 128))
    for t in range(4):
        value = source[:, 128 * t : 128 * t + 128] * scale
        other = swap(value)
        rows_by_load[pl.ds(2 * t, ROWS, stride=8), :] = jnp.where(mask, value, other)
        rows_by_load[pl.ds(2 * t + 1, ROWS, stride=8), :] = jnp.where(mask, other, value)


def update_step(q, product, residual_in, direction_in, solution_in, factors, outs):
    residual = residual_in - product
    if factors is None:
        direction = residual / CENTER
    else:
        direction = factors[0] * direction_in + factors[1] * residual
    outs[0][q] = residual
    outs[1][q] = direction
    outs[2][q] = solution_in + direction


def first_one_kernel(
    flags, ghosts, index_ref, send_ref, mine, left, right, high_ref, low_ref,
    rhs_out, r_out, d_out, x_out, to_left, to_right, table, by_load,
):
    base = 72
    mask = low_lanes((8, 128))

    def row(r):
        return by_load[pl.ds(pl.multiple_of(8 * r, 8), 8), :]

    unpack_natural(mine, by_load, 1.0)

    def own(q):
        value = jnp.where(mask, row(2 * q), row(2 * q + 1))
        rhs_out[q] = value
        return value / CENTER

    fill_table(table, 12, 48, base, own)
    for side, source, start in ((0, left, 0), (1, right, 60)):
        keep = flags[side] > 0
        unpack_natural(source, by_load, 1.0)

        def ghost(q):
            at = side * GHOST + 2 * q
            value = jnp.where(mask, row(ghosts[at]), row(ghosts[at + 1])) / CENTER
            return jnp.where(keep, value, jnp.zeros_like(value))

        fill_table(table, start, 12, base, ghost)

    def step(g):
        products = operator_group(table, base, 12, g, index_ref, ROWS, high_ref, low_ref)
        for j in range(2):
            q = 2 * g + j
            direction = table[12 + q]
            update_step(
                q, products[j], rhs_out[q], direction, direction, FACTORS[0], (r_out, d_out, x_out)
            )

    each(24, step)
    gather_sends(d_out, send_ref, to_left, to_right)


def fill_one(flags, vector, left, right, table):
    base = 72
    fill_table(table, 12, 48, base, lambda q: vector[q])
    for side, source, start in ((0, left, 0), (1, right, 60)):
        keep = flags[side] > 0
        fill_table(
            table, start, 12, base,
            lambda q: jnp.where(keep, source[q], jnp.zeros((8, 128), f32)),
        )


def one_kernel(
    flags, index_ref, send_ref, vector, left, right, residual, solution, high_ref, low_ref,
    r_out, d_out, x_out, to_left, to_right, table, *, factors,
):
    fill_one(flags, vector, left, right, table)

    def step(g):
        products = operator_group(table, 72, 12, g, index_ref, ROWS, high_ref, low_ref)
        for j in range(2):
            q = 2 * g + j
            start = vector[q] if solution is None else solution[q]
            update_step(
                q, products[j], residual[q], vector[q], start, factors, (r_out, d_out, x_out)
            )

    each(24, step)
    gather_sends(d_out, send_ref, to_left, to_right)


def restrict_one_kernel(
    flags, index_ref, agg_ref, vector, left, right, residual, high_ref, low_ref, prol_h, prol_l,
    out, table, sums,
):
    fill_one(flags, vector, left, right, table)
    zero_sums(sums, ROWS)

    def step(g):
        products = operator_group(table, 72, 12, g, index_ref, ROWS, high_ref, low_ref)
        finals = [residual[2 * g + j] - products[j] for j in range(2)]
        restrict_group(finals[0], finals[1], g, agg_ref, prol_h, prol_l, sums)

    each(24, step)
    pack_sums(sums, out, ROWS)


def last_one_kernel(
    flags, index_ref, vector, left, right, residual, solution, high_ref, low_ref,
    out, table, by_load,
):
    fill_one(flags, vector, left, right, table)
    factors = FACTORS[1]

    def step(g):
        products = operator_group(table, 72, 12, g, index_ref, ROWS, high_ref, low_ref)
        for j in range(2):
            q = 2 * g + j
            direction = factors[0] * vector[q] + factors[1] * (residual[q] - products[j])
            value = solution[q] + direction
            by_load[pl.ds(pl.multiple_of(16 * q, 16), 8), :] = value
            by_load[pl.ds(pl.multiple_of(16 * q + 8, 8), 8), :] = swap(value)

    each(24, step)
    pack_natural(by_load, out, ROWS)


def pack_natural(by_load, out, rows):
    mask = low_lanes((rows, 128))
    for t in range(4):
        even = by_load[pl.ds(2 * t, rows, stride=8), :]
        odd = by_load[pl.ds(2 * t + 1, rows, stride=8), :]
        out[:, 128 * t : 128 * t + 128] = jnp.where(mask, even, swap(odd))


def fill_two(flags, vector, left, right, table, scale):
    base = 144
    for side, source, start in ((0, left, 0), (None, vector, 48), (1, right, 96)):
        if side is None:
            read = lambda q: source[q] / CENTER if scale else source[q]
        else:
            keep = flags[side] > 0

            def read(q):
                value = source[q] / CENTER if scale else source[q]
                return jnp.where(keep, value, jnp.zeros_like(value))

        fill_table(table, start, 48, base, read)


def two_kernel(
    flags, index_ref, vector, left, right, residual, solution, high_ref, low_ref,
    r_out, d_out, x_out, table, *, factors, scale,
):
    fill_two(flags, vector, left, right, table, scale)

    def step(g):
        products = operator_group(table, 144, 48, g, index_ref, ROWS, high_ref, low_ref)
        for j in range(2):
            q = 2 * g + j
            direction = table[48 + q]
            start = direction if solution is None else solution[q]
            update_step(
                q, products[j], residual[q], direction, start, factors, (r_out, d_out, x_out)
            )

    each(24, step)


def restrict_two_kernel(
    flags, index_ref, agg_ref, vector, left, right, residual, high_ref, low_ref, prol_h, prol_l,
    out, table, sums,
):
    fill_two(flags, vector, left, right, table, False)
    zero_sums(sums, COARSE)

    def step(g):
        products = operator_group(table, 144, 48, g, index_ref, ROWS, high_ref, low_ref)
        finals = [residual[2 * g + j] - products[j] for j in range(2)]
        restrict_group(finals[0], finals[1], g, agg_ref, prol_h, prol_l, sums)

    each(12, step)
    pack_sums(sums, out, COARSE)


def coarse_kernel(
    index_ref, agg_ref, rhs, smooth, high_ref, low_ref, own_h, own_l, other_h, other_l,
    natural_out, corrected_out, table, residual, direction, coarse_out, by_load,
):
    base = COARSE // 2

    def start(q):
        value = rhs[q]
        residual[q] = value
        direction[q] = value / CENTER
        coarse_out[q] = value / CENTER

    each(base, start)
    for factors in FACTORS:
        fill_table(table, 0, base, base, lambda q: direction[q])

        def step(g):
            products = operator_group(table, base, 0, g, index_ref, COARSE, high_ref, low_ref)
            for j in range(2):
                q = 2 * g + j
                now = residual[q] - products[j]
                residual[q] = now
                turned = factors[0] * direction[q] + factors[1] * now
                direction[q] = turned
                coarse_out[q] = coarse_out[q] + turned

        each(COARSE // 4, step)
    fill_table(table, 0, base, base, lambda q: coarse_out[q])
    for start_g, high_p, low_p in ((0, own_h, own_l), (12, other_h, other_l)):

        def lift(g):
            products = prolong_group(table, base, g, agg_ref, high_p, low_p, 4 * start_g)
            for j in range(2):
                q = 2 * (start_g + g) + j
                corrected_out[q] = smooth[q] + products[j]

        each(12, lift)
    for q in range(base):
        by_load[16 * q : 16 * q + 8, :] = table[q]
        by_load[16 * q + 8 : 16 * q + 16, :] = table[base + q]
    pack_natural(by_load, natural_out, COARSE)


def lift_kernel(
    flags, index_ref, agg_ref, send_ref, vector, left, right, residual, solution, smooth, high_ref,
    low_ref, prol_h, prol_l, corrected_out, to_left, to_right, table, lifted,
):
    fill_two(flags, vector, left, right, table, False)
    factors = FACTORS[1]

    def step(g):
        products = operator_group(table, 144, 48, g, index_ref, ROWS, high_ref, low_ref)
        for j in range(2):
            q = 2 * g + j
            direction = factors[0] * table[48 + q] + factors[1] * (residual[q] - products[j])
            value = solution[q] + direction
            lifted[q] = value
            lifted[48 + q] = swap(value)

    each(24, step)

    def lift(g):
        products = prolong_group(lifted, 48, g, agg_ref, prol_h, prol_l, 0)
        for j in range(2):
            q = 2 * g + j
            corrected_out[q] = smooth[q] + products[j]

    each(24, lift)
    gather_sends(corrected_out, send_ref, to_left, to_right)


def packed(pairs):
    return jax.ShapeDtypeStruct((pairs, 8, 128), f32)


class Streamed:
    def __init__(self, sources, buffer, semaphores):
        self.buffer = buffer
        self.copies = []
        start = 0
        for source in sources:
            groups = source.shape[0]
            pieces = 2 if groups >= 12 else 1
            for piece in range(pieces):
                count = groups // pieces
                self.copies.append(
                    (
                        start,
                        pltpu.make_async_copy(
                            source.at[pl.ds(piece * count, count)],
                            buffer.at[pl.ds(start, count)],
                            semaphores.at[len(self.copies)],
                        ),
                    )
                )
                start += count
        self.copies = [c for c in self.copies if c[0] < buffer.shape[0]]

    def __getitem__(self, group):
        while self.copies and self.copies[0][0] <= group:
            self.copies.pop(0)[1].wait()
        return self.buffer[group]


class Parts:
    def __init__(self, refs):
        self.refs = refs

    def __getitem__(self, group):
        for ref in self.refs:
            if group < ref.shape[0]:
                return ref[group]
            group -= ref.shape[0]


def order_spec(array):
    return SM if array.dtype == jnp.int32 else pl.BlockSpec(memory_space=pl.ANY)


def call(
    kernel, scalars, arrays, weights, outs, scratch, weight, token=False, after=(), carry=None
):
    single = not isinstance(outs, tuple)
    if single:
        outs = (outs,)
    parts = [p for w in weights for p in w]
    inputs, results = len(scalars) + len(arrays), len(outs)

    def run(*refs):
        first, refs = refs[:inputs], refs[inputs:]
        sources, refs = refs[: len(parts)], refs[len(parts) :]
        rest = refs[len(after) :]
        if carry is not None:
            carried, rest = rest[0], rest[1:]
        results_refs, rest = rest[:results], rest[results:]
        if token:
            rest[0][0] = 0
            rest = rest[1:]
        copy = None
        if carry is not None:
            out, semaphore = rest[0], rest[-1]
            rest = rest[1:-1]
            copy = pltpu.make_async_copy(
                carried.at[pl.ds(carry[1], carry[2])], out, semaphore
            )
            copy.start()
        held, at = [], 0
        for w in weights:
            held.append(Parts(sources[at : at + len(w)]))
            at += len(w)
        kernel(*first, *held, *results_refs, *rest)
        if copy is not None:
            copy.wait()

    out_shape = tuple(outs) + ((jax.ShapeDtypeStruct((1,), jnp.int32),) if token else ())
    out_specs = (VM,) * results + ((SM,) if token else ())
    scratch_shapes = [pltpu.VMEM(shape, f32) for shape in scratch]
    in_specs = [SM] * len(scalars) + [VM] * (len(arrays) + len(parts)) + [order_spec(a) for a in after]
    extra = ()
    if carry is not None:
        array, _, count = carry
        extra = (array,)
        shape = (count,) + array.shape[1:]
        out_shape += (jax.ShapeDtypeStruct(shape, array.dtype),)
        out_specs += (pl.BlockSpec(memory_space=pl.ANY),)
        in_specs.append(pl.BlockSpec(memory_space=pl.ANY))
        scratch_shapes.append(pltpu.SemaphoreType.DMA)
    got = pl.pallas_call(
        run,
        out_shape=out_shape,
        in_specs=in_specs,
        out_specs=out_specs,
        scratch_shapes=scratch_shapes,
        compiler_params=pltpu.CompilerParams(vmem_limit_bytes=VMEM_LIMIT),
        cost_estimate=pl.CostEstimate(
            flops=weight * 10**9, bytes_accessed=8 * 2**20, transcendentals=0
        ),
    )(*scalars, *arrays, *parts, *after, *extra)
    return got[0] if single else got


def drop(kernel, position, **options):
    def run(*refs):
        return kernel(*refs[:position], None, *refs[position:], **options)

    return run


def exchange(value, pairs):
    return lax.ppermute(value, AXES, pairs)


def high_half(rows):
    return 1 - (rows & 1), rows >> 1


def body(
    right_side, ghost_rows, cols_one, diag_one, offd_one, prol_one, agg_one, cols_two, diag_two,
    offd_two, prol_two, agg_two, cols_three, diag_three, offd_three,
):
    blocks = lax.axis_size("grp") * lax.axis_size("dev")
    block = lax.axis_index("grp") * lax.axis_size("dev") + lax.axis_index("dev")
    half = block % 2
    pair = block // 2

    def shift(value, steps):
        return exchange(value, [(s, (s + steps) % blocks) for s in range(blocks)])

    def flip(value, mask):
        return exchange(value, [(s, s ^ mask) for s in range(blocks)])

    left_raw = shift(right_side, 1)
    right_raw = shift(right_side, -1)
    lists = jnp.concatenate([shift(ghost_rows[1], 1), shift(ghost_rows[0], -1)])

    flags_one = jnp.stack([block > 0, block < blocks - 1]).astype(jnp.int32)
    flags_two = jnp.stack([pair > 0, pair < blocks // 2 - 1]).astype(jnp.int32)

    def slots(first, second, base):
        return jnp.concatenate(
            [(1 - (first & 1)) * base + (first >> 1), (second & 1) * base + (second >> 1)]
        )

    def low_slot(rows, base):
        return (rows & 1) * base + (rows >> 1)

    def local_row(rows):
        return (rows + half * HALF) % ROWS

    index_one = slots(cols_one[:, 0], cols_one[:, 1], 72)
    numbers = flip(jnp.concatenate([cols_two.reshape(-1), agg_two]), 1)
    cols_pair = jnp.concatenate([cols_two, numbers[: 2 * HALF].reshape(HALF, 2)], 0)
    cols_pair = (cols_pair // ROWS) * ROWS + local_row(cols_pair % ROWS)
    index_two = slots(cols_pair[:, 0], cols_pair[:, 1], 144)
    index_three = slots(cols_three[:, 0], cols_three[:, 1], COARSE // 2)
    agg_pair = low_slot(jnp.concatenate([agg_two, numbers[2 * HALF :]]), COARSE // 2)
    agg_local = local_row(agg_one)
    lift_index = low_slot(agg_local, 48)

    def paired(prepared):
        return tuple((w,) for w in prepared[:2])

    own_list = ghost_rows.reshape(-1)
    numbers_one = (flags_one, own_list, index_one, lists, agg_local, lift_index)
    numbers_two = (flags_two, index_two, index_three, agg_pair)
    one_w = paired(prepare((diag_one, offd_one), ROWS, after=numbers_one + numbers_two))
    diag_other = flip(diag_two, 1)

    v48, v12 = packed(48), packed(12)
    table_one, table_two = (144, 8, 128), (288, 8, 128)
    by_load = (ROWS * 8, 128)

    rhs, r, d, x, to_left, to_right, token, offd_a = call(
        first_one_kernel,
        (flags_one, own_list, index_one, lists),
        (right_side, left_raw, right_raw),
        one_w,
        (v48, v48, v48, v48, v12, v12),
        (table_one, by_load),
        2,
        token=True,
        after=(diag_other,),
        carry=(offd_two, 0, 24),
    )
    other_a = prepare((diag_other, flip(offd_a, 1)), 24)
    prol_one_ready = prepare((prol_one,), ROWS, after=(token,))
    one_p = paired(prol_one_ready)
    two_own = prepare((diag_two, offd_two), HALF, after=(token,))

    def one_turn(d, r, x, to_left, to_right, factors, after=(), carry=None):
        from_left, from_right = shift(to_right, 1), shift(to_left, -1)
        return call(
            functools.partial(one_kernel, factors=factors),
            (flags_one, index_one, lists),
            (d, from_left, from_right, r, x),
            one_w,
            (v48, v48, v48, v12, v12),
            (table_one,),
            2,
            after=after,
            carry=carry,
        )

    r, d, smooth_one, to_left, to_right, offd_b = one_turn(
        d, r, x, to_left, to_right, FACTORS[1],
        after=(prol_one_ready[2], two_own[2], other_a[2]),
        carry=(offd_two, 24, 24),
    )
    other_b = prepare((diag_other, flip(offd_b, 1)), 24, start=24)
    two_w = tuple((two_own[k], other_a[k], other_b[k]) for k in range(2))
    part = call(
        restrict_one_kernel,
        (flags_one, index_one, agg_local),
        (d, shift(to_right, 1), shift(to_left, -1), r),
        (*one_w, *one_p),
        v48,
        (table_one, (ROWS, 8, 128)),
        3,
    )
    rhs_two = combine(part, flip(part, 1))

    def two_turn(d, r, x, factors, scale=False, token=False, after=()):
        from_left, from_right = shift(d, 2), shift(d, -2)
        kernel = functools.partial(two_kernel, factors=factors, scale=scale)
        arrays = [d, from_left, from_right, r]
        if x is None:
            kernel = drop(two_kernel, 6, factors=factors, scale=scale)
        else:
            arrays.append(x)
        return call(
            kernel,
            (flags_two, index_two),
            arrays,
            two_w,
            (v48, v48, v48),
            (table_two,),
            2,
            token=token,
            after=after,
        )

    r, d, x, token = two_turn(rhs_two, rhs_two, None, FACTORS[0], scale=True, token=True)
    three_ready = prepare((diag_three, offd_three), COARSE, after=(token,))
    three_w = paired(three_ready)
    r, d, smooth_two, token = two_turn(
        d, r, x, FACTORS[1], token=True, after=(three_ready[2],)
    )
    two_p = paired(prepare((prol_two,), HALF, after=(token,)))
    two_p_other = paired(prepare((flip(prol_two, 1),), HALF, after=(token,)))
    coarse_rhs = call(
        restrict_two_kernel,
        (flags_two, index_two, agg_two),
        (d, shift(d, 2), shift(d, -2), r),
        (*[w[:1] for w in two_w], *two_p),
        packed(COARSE // 2),
        (table_two, (COARSE, 8, 128)),
        2,
    )
    for masks in reduce_phases(blocks):
        others = [flip(coarse_rhs, m) for m in masks]
        if len(masks) == 1:
            coarse_rhs = coarse_rhs + others[0]
        else:
            coarse_rhs = (coarse_rhs + others[0]) + (others[1] + others[2])

    coarse_solution, corrected_two = call(
        coarse_kernel,
        (index_three, agg_pair),
        (coarse_rhs, smooth_two),
        (*three_w, *two_p, *two_p_other),
        (jax.ShapeDtypeStruct((COARSE, LOADS * TILE), f32), v48),
        (
            (COARSE, 8, 128),
            (COARSE // 2, 8, 128),
            (COARSE // 2, 8, 128),
            (COARSE // 2, 8, 128),
            (COARSE * 8, 128),
        ),
        4,
    )

    r, d, x = two_turn(corrected_two, rhs_two, corrected_two, None)
    r, d, x = two_turn(d, r, x, FACTORS[0])
    corrected_one, to_left, to_right = call(
        lift_kernel,
        (flags_two, index_two, lift_index, lists),
        (d, shift(d, 2), shift(d, -2), r, x, smooth_one),
        (*two_w, *one_p),
        (v48, v12, v12),
        (table_two, (ROWS, 8, 128)),
        3,
    )

    r, d, x, to_left, to_right = one_turn(
        corrected_one, rhs, corrected_one, to_left, to_right, None
    )
    r, d, x, to_left, to_right = one_turn(d, r, x, to_left, to_right, FACTORS[0])
    solution = call(
        last_one_kernel,
        (flags_one, index_one),
        (d, shift(to_right, 1), shift(to_left, -1), r, x),
        one_w,
        jax.ShapeDtypeStruct((ROWS, LOADS * TILE), f32),
        (table_one, by_load),
        2,
    )
    return solution, coarse_solution


def reduce_phases(blocks):
    if blocks == 256:
        return ((32,), (4,), (8, 16, 24), (64, 128, 192), (1, 2, 3))
    return tuple((1 << bit,) for bit in range(blocks.bit_length() - 1))


def solution(mesh):
    rows = P(AXES, None)
    return jax.shard_map(
        body,
        mesh=mesh,
        in_specs=(
            rows, rows, rows, rows, P(AXES, None, None), rows, P(AXES), rows, rows,
            P(AXES, None, None), rows, P(AXES), P(), P(), P(),
        ),
        out_specs=(rows, P()),
        check_vma=False,
    )
```

```python
import functools

import jax
import jax.numpy as jnp
from jax import lax
from jax.experimental import pallas as pl
from jax.experimental.pallas import tpu as pltpu
from jax.sharding import PartitionSpec as P

TILE = 64
LOADS = 8
ROWS = 96
HALF = 48
COARSE = 32
GHOST = 24
AXES = ("grp", "dev")
VMEM_LIMIT = 8 * 2**20

CENTER = 5.0
RADIUS = 4.0
SIGMA = 1.25

bf16 = jnp.bfloat16
f32 = jnp.float32
VM = pl.BlockSpec(memory_space=pltpu.VMEM)
SM = pl.BlockSpec(memory_space=pltpu.SMEM)


def chebyshev_factors(count):
    rho = 1.0 / SIGMA
    factors = []
    for _ in range(count):
        rho_next = 1.0 / (2.0 * SIGMA - rho)
        factors.append((rho_next * rho, 2.0 * rho_next / RADIUS))
        rho = rho_next
    return factors


FACTORS = chebyshev_factors(7)


def low_lanes(shape):
    return lax.broadcasted_iota(jnp.int32, shape, len(shape) - 1) < TILE


def swap(value):
    return pltpu.roll(value, TILE, value.ndim - 1)


def each(count, step):
    for at in range(count):
        step(at)


def split(value):
    high = value.astype(bf16)
    return high, (value - high.astype(f32)).astype(bf16)


def dot_nt(a, b):
    return lax.dot_general(a, b, (((1,), (1,)), ((), ())), preferred_element_type=f32)


def dot_nn(a, b):
    return lax.dot_general(a, b, (((1,), (0,)), ((), ())), preferred_element_type=f32)


def fill_table(table, start, count, base, read):
    for q in range(count):
        value = read(q)
        table[start + q] = value
        table[base + start + q] = swap(value)


def block_products(left, high_w, low_w):
    high, low = split(left)
    both = dot_nn(jnp.concatenate([high, low], 0), high_w)
    rest = dot_nn(high, low_w)
    mask = low_lanes((8, 128))

    def block(i):
        lanes = slice((i // 2) * 128, (i // 2) * 128 + 128)
        return (
            both[8 * i : 8 * i + 8, lanes]
            + both[32 + 8 * i : 40 + 8 * i, lanes]
            + rest[8 * i : 8 * i + 8, lanes]
        )

    return [jnp.where(mask, block(2 * j), block(2 * j + 1)) for j in range(2)]


def operator_group(table, base, own, g, index_ref, count, high_ref, low_ref):
    mask = low_lanes((8, 128))
    rows = []
    for i in range(4):
        mine = table[(i & 1) * base + own + 2 * g + (i >> 1)]
        first = table[index_ref[4 * g + i]]
        second = table[index_ref[count + 4 * g + i]]
        rows.append(jnp.concatenate([jnp.where(mask, mine, first), second], 1))
    left = jnp.concatenate(rows, 0)[:, : 3 * TILE]
    return block_products(left, high_ref[g], low_ref[g])


def prolong_group(table, base, g, index_ref, high_ref, low_ref, row_start):
    rows = [table[index_ref[row_start + 4 * g + i]] for i in range(4)]
    left = jnp.concatenate(rows, 0)[:, :TILE]
    return block_products(left, high_ref[g], low_ref[g])


def restrict_group(pair0, pair1, g, agg_ref, high_ref, low_ref, sums):
    mask = low_lanes((8, 128))
    zero = jnp.zeros((8, 128), f32)
    rows = [
        jnp.concatenate([jnp.where(mask, pair0, zero), zero], 1),
        jnp.concatenate([jnp.where(mask, zero, pair0), zero], 1),
        jnp.concatenate([zero, jnp.where(mask, pair1, zero)], 1),
        jnp.concatenate([zero, jnp.where(mask, zero, pair1)], 1),
    ]
    high, low = split(jnp.concatenate(rows, 0))
    both = dot_nt(jnp.concatenate([high, low], 0), high_ref[g])
    terms = both[:32] + both[32:] + dot_nt(high, low_ref[g])
    for i in range(4):
        row = agg_ref[4 * g + i]
        sums[i][row, :, :TILE] = sums[i][row, :, :TILE] + terms[8 * i : 8 * i + 8]


def zero_sums(sums, count):
    for total in sums:
        for q in range(count):
            total[q] = jnp.zeros((8, 128), f32)


def pack_sums(sums, out, count):
    def row(r):
        return (sums[0][r] + sums[1][r]) + (sums[2][r] + sums[3][r])

    for q in range(count // 2):
        out[q] = row(2 * q) + swap(row(2 * q + 1))


def gather_sends(vector, send_ref, to_left, to_right):
    mask = low_lanes((8, 128))

    def half(row, odd):
        value = vector[row >> 1]
        return jnp.where((row & 1) == odd, value, swap(value))

    def step(q):
        for side, out in ((0, to_left), (1, to_right)):
            at = side * GHOST + 2 * q
            out[q] = jnp.where(mask, half(send_ref[at], 0), half(send_ref[at + 1], 1))

    each(GHOST // 2, step)


PITCH = 72


def prepare_operator_kernel(diag_ref, offd_ref, high_ref, low_ref, token, stage_a, stage_b):
    token[0] = 0
    mask = low_lanes((8, 128))
    for s in range(32):
        lanes = slice(128 * s, 128 * s + 128)
        diag, first, second = diag_ref[:, lanes], offd_ref[:, 0, lanes], offd_ref[:, 1, lanes]
        even, odd = pl.ds(2 * s, 8, stride=PITCH), pl.ds(2 * s + 1, 8, stride=PITCH)
        stage_a[even, :] = jnp.where(mask, diag, swap(first))
        stage_a[odd, :] = jnp.where(mask, swap(diag), first)
        stage_b[even, :] = second
        stage_b[odd, :] = swap(second)
    store_turned(((stage_a, 128, 0), (stage_b, 64, 128)), high_ref, low_ref)


def store_turned(stages, high_ref, low_ref):
    for j in range(2):
        for stage, count, at in stages:
            rows = [stage[pl.ds(PITCH * (4 * j + i), TILE), :] for i in range(4)]
            high, low = split(jnp.concatenate(rows, 0).T[:count])
            high_ref[j, at : at + count, :] = high
            low_ref[j, at : at + count, :] = low


def prepare_transfer_kernel(prol_ref, high_ref, low_ref, token, stage):
    token[0] = 0
    for s in range(32):
        prol = prol_ref[:, 128 * s : 128 * s + 128]
        stage[pl.ds(2 * s, 8, stride=PITCH), :] = prol
        stage[pl.ds(2 * s + 1, 8, stride=PITCH), :] = swap(prol)
    store_turned(((stage, 64, 0),), high_ref, low_ref)


def prepare(tile_arrays, rows, start=0, after=(), carry=None):
    operator = len(tile_arrays) == 2
    depth = 3 * TILE if operator else TILE
    out = jax.ShapeDtypeStruct((rows // 4, depth, 256), bf16)
    out_spec = pl.BlockSpec((2, depth, 256), lambda g: (g, 0, 0))
    first = start // 8
    specs = [pl.BlockSpec((8, 4096), lambda g: (g + first, 0))]
    if operator:
        specs.append(pl.BlockSpec((8, 2, 4096), lambda g: (g, 0, 0)))
    kernel = prepare_operator_kernel if operator else prepare_transfer_kernel
    out_shape = (out, out, jax.ShapeDtypeStruct((1,), jnp.int32))
    out_specs = (out_spec, out_spec, SM)
    scratch_shapes = [pltpu.VMEM((8 * PITCH, 128), f32)] * (2 if operator else 1)
    if carry is not None:
        array, carry_start, count = carry
        out_shape += (jax.ShapeDtypeStruct((count,) + array.shape[1:], array.dtype),)
        out_specs += (pl.BlockSpec(memory_space=pl.ANY),)
        scratch_shapes.append(pltpu.SemaphoreType.DMA)
        after = (array,) + tuple(after)

    def run(*refs):
        arguments = list(refs[len(after) :])
        if carry is None:
            return kernel(*arguments)
        semaphore = arguments.pop()
        target = arguments.pop(len(tile_arrays) + 3)
        copy = pltpu.make_async_copy(refs[0].at[pl.ds(carry_start, count)], target, semaphore)
        pl.when(pl.program_id(0) == 0)(copy.start)
        kernel(*arguments)
        pl.when(pl.program_id(0) == rows // 8 - 1)(copy.wait)

    return pl.pallas_call(
        run,
        out_shape=out_shape,
        grid=(rows // 8,),
        in_specs=[order_spec(a) for a in after] + specs,
        out_specs=out_specs,
        scratch_shapes=scratch_shapes,
        compiler_params=pltpu.CompilerParams(vmem_limit_bytes=VMEM_LIMIT),
        cost_estimate=pl.CostEstimate(
            flops=rows * (8 if operator else 4) * 10**7,
            bytes_accessed=rows * (98304 if operator else 32768),
            transcendentals=0,
        ),
    )(*after, *tile_arrays)


def combine_kernel(mine, other, out):
    for q in range(HALF):
        out[q] = mine[q] + other[(q + 24) % 48]


def combine(mine, other):
    return pl.pallas_call(
        combine_kernel,
        out_shape=packed(48),
        in_specs=[VM, VM],
        out_specs=VM,
        compiler_params=pltpu.CompilerParams(vmem_limit_bytes=VMEM_LIMIT),
    )(mine, other)


def unpack_natural(source, rows_by_load, scale):
    mask = low_lanes((ROWS, 128))
    for t in range(4):
        value = source[:, 128 * t : 128 * t + 128] * scale
        other = swap(value)
        rows_by_load[pl.ds(2 * t, ROWS, stride=8), :] = jnp.where(mask, value, other)
        rows_by_load[pl.ds(2 * t + 1, ROWS, stride=8), :] = jnp.where(mask, other, value)


def update_step(q, product, residual_in, direction_in, solution_in, factors, outs):
    residual = residual_in - product
    if factors is None:
        direction = residual / CENTER
    else:
        direction = factors[0] * direction_in + factors[1] * residual
    outs[0][q] = residual
    outs[1][q] = direction
    outs[2][q] = solution_in + direction


def first_one_kernel(
    flags, ghosts, index_ref, send_ref, mine, left, right, high_ref, low_ref,
    rhs_out, r_out, d_out, x_out, to_left, to_right, table, by_load,
):
    base = 72
    mask = low_lanes((8, 128))

    def row(r):
        return by_load[pl.ds(pl.multiple_of(8 * r, 8), 8), :]

    unpack_natural(mine, by_load, 1.0)

    def own(q):
        value = jnp.where(mask, row(2 * q), row(2 * q + 1))
        rhs_out[q] = value
        return value / CENTER

    fill_table(table, 12, 48, base, own)
    for side, source, start in ((0, left, 0), (1, right, 60)):
        keep = flags[side] > 0
        unpack_natural(source, by_load, 1.0)

        def ghost(q):
            at = side * GHOST + 2 * q
            value = jnp.where(mask, row(ghosts[at]), row(ghosts[at + 1])) / CENTER
            return jnp.where(keep, value, jnp.zeros_like(value))

        fill_table(table, start, 12, base, ghost)

    def step(g):
        products = operator_group(table, base, 12, g, index_ref, ROWS, high_ref, low_ref)
        for j in range(2):
            q = 2 * g + j
            direction = table[12 + q]
            update_step(
                q, products[j], rhs_out[q], direction, direction, FACTORS[0], (r_out, d_out, x_out)
            )

    each(24, step)
    gather_sends(d_out, send_ref, to_left, to_right)


def fill_one(flags, vector, left, right, table):
    base = 72
    fill_table(table, 12, 48, base, lambda q: vector[q])
    for side, source, start in ((0, left, 0), (1, right, 60)):
        keep = flags[side] > 0
        fill_table(
            table, start, 12, base,
            lambda q: jnp.where(keep, source[q], jnp.zeros((8, 128), f32)),
        )


def one_kernel(
    flags, index_ref, send_ref, vector, left, right, residual, solution, high_ref, low_ref,
    r_out, d_out, x_out, to_left, to_right, table, *, factors,
):
    fill_one(flags, vector, left, right, table)

    def step(g):
        products = operator_group(table, 72, 12, g, index_ref, ROWS, high_ref, low_ref)
        for j in range(2):
            q = 2 * g + j
            start = vector[q] if solution is None else solution[q]
            update_step(
                q, products[j], residual[q], vector[q], start, factors, (r_out, d_out, x_out)
            )

    each(24, step)
    gather_sends(d_out, send_ref, to_left, to_right)


def restrict_one_kernel(
    flags, index_ref, agg_ref, vector, left, right, residual, high_ref, low_ref, prol_h, prol_l,
    out, table, *sums,
):
    fill_one(flags, vector, left, right, table)
    zero_sums(sums, ROWS)

    def step(g):
        products = operator_group(table, 72, 12, g, index_ref, ROWS, high_ref, low_ref)
        finals = [residual[2 * g + j] - products[j] for j in range(2)]
        restrict_group(finals[0], finals[1], g, agg_ref, prol_h, prol_l, sums)

    each(24, step)
    pack_sums(sums, out, ROWS)


def last_one_kernel(
    flags, index_ref, vector, left, right, residual, solution, high_ref, low_ref,
    out, table, by_load,
):
    fill_one(flags, vector, left, right, table)
    factors = FACTORS[1]

    def step(g):
        products = operator_group(table, 72, 12, g, index_ref, ROWS, high_ref, low_ref)
        for j in range(2):
            q = 2 * g + j
            direction = factors[0] * vector[q] + factors[1] * (residual[q] - products[j])
            value = solution[q] + direction
            by_load[pl.ds(pl.multiple_of(16 * q, 16), 8), :] = value
            by_load[pl.ds(pl.multiple_of(16 * q + 8, 8), 8), :] = swap(value)

    each(24, step)
    pack_natural(by_load, out, ROWS)


def pack_natural(by_load, out, rows):
    mask = low_lanes((rows, 128))
    for t in range(4):
        even = by_load[pl.ds(2 * t, rows, stride=8), :]
        odd = by_load[pl.ds(2 * t + 1, rows, stride=8), :]
        out[:, 128 * t : 128 * t + 128] = jnp.where(mask, even, swap(odd))


def fill_two(flags, vector, left, right, table, scale):
    base = 144
    for side, source, start in ((0, left, 0), (None, vector, 48), (1, right, 96)):
        if side is None:
            read = lambda q: source[q] / CENTER if scale else source[q]
        else:
            keep = flags[side] > 0

            def read(q):
                value = source[q] / CENTER if scale else source[q]
                return jnp.where(keep, value, jnp.zeros_like(value))

        fill_table(table, start, 48, base, read)


def two_kernel(
    flags, index_ref, vector, left, right, residual, solution, high_ref, low_ref,
    r_out, d_out, x_out, table, *, factors, scale,
):
    fill_two(flags, vector, left, right, table, scale)

    def step(g):
        products = operator_group(table, 144, 48, g, index_ref, ROWS, high_ref, low_ref)
        for j in range(2):
            q = 2 * g + j
            direction = table[48 + q]
            start = direction if solution is None else solution[q]
            update_step(
                q, products[j], residual[q], direction, start, factors, (r_out, d_out, x_out)
            )

    each(24, step)


def restrict_two_kernel(
    flags, index_ref, agg_ref, vector, left, right, residual, high_ref, low_ref, prol_h, prol_l,
    out, table, *sums,
):
    fill_two(flags, vector, left, right, table, False)
    zero_sums(sums, COARSE)

    def step(g):
        products = operator_group(table, 144, 48, g, index_ref, ROWS, high_ref, low_ref)
        finals = [residual[2 * g + j] - products[j] for j in range(2)]
        restrict_group(finals[0], finals[1], g, agg_ref, prol_h, prol_l, sums)

    each(12, step)
    pack_sums(sums, out, COARSE)


def coarse_kernel(
    index_ref, agg_ref, rhs, smooth, high_ref, low_ref, own_h, own_l, other_h, other_l,
    natural_out, corrected_out, table, residual, direction, coarse_out, by_load,
):
    base = COARSE // 2

    def start(q):
        value = rhs[q]
        residual[q] = value
        direction[q] = value / CENTER
        coarse_out[q] = value / CENTER

    each(base, start)
    for factors in FACTORS:
        fill_table(table, 0, base, base, lambda q: direction[q])

        def step(g):
            products = operator_group(table, base, 0, g, index_ref, COARSE, high_ref, low_ref)
            for j in range(2):
                q = 2 * g + j
                now = residual[q] - products[j]
                residual[q] = now
                turned = factors[0] * direction[q] + factors[1] * now
                direction[q] = turned
                coarse_out[q] = coarse_out[q] + turned

        each(COARSE // 4, step)
    fill_table(table, 0, base, base, lambda q: coarse_out[q])
    for start_g, high_p, low_p in ((0, own_h, own_l), (12, other_h, other_l)):

        def lift(g):
            products = prolong_group(table, base, g, agg_ref, high_p, low_p, 4 * start_g)
            for j in range(2):
                q = 2 * (start_g + g) + j
                corrected_out[q] = smooth[q] + products[j]

        each(12, lift)
    for q in range(base):
        by_load[16 * q : 16 * q + 8, :] = table[q]
        by_load[16 * q + 8 : 16 * q + 16, :] = table[base + q]
    pack_natural(by_load, natural_out, COARSE)


def lift_kernel(
    flags, index_ref, agg_ref, send_ref, vector, left, right, residual, solution, smooth, high_ref,
    low_ref, prol_h, prol_l, corrected_out, to_left, to_right, table, lifted,
):
    fill_two(flags, vector, left, right, table, False)
    factors = FACTORS[1]

    def step(g):
        products = operator_group(table, 144, 48, g, index_ref, ROWS, high_ref, low_ref)
        for j in range(2):
            q = 2 * g + j
            direction = factors[0] * table[48 + q] + factors[1] * (residual[q] - products[j])
            value = solution[q] + direction
            lifted[q] = value
            lifted[48 + q] = swap(value)

    each(24, step)

    def lift(g):
        products = prolong_group(lifted, 48, g, agg_ref, prol_h, prol_l, 0)
        for j in range(2):
            q = 2 * g + j
            corrected_out[q] = smooth[q] + products[j]

    each(24, lift)
    gather_sends(corrected_out, send_ref, to_left, to_right)


def packed(pairs):
    return jax.ShapeDtypeStruct((pairs, 8, 128), f32)


class Streamed:
    def __init__(self, sources, buffer, semaphores):
        self.buffer = buffer
        self.copies = []
        start = 0
        for source in sources:
            groups = source.shape[0]
            pieces = 2 if groups >= 12 else 1
            for piece in range(pieces):
                count = groups // pieces
                self.copies.append(
                    (
                        start,
                        pltpu.make_async_copy(
                            source.at[pl.ds(piece * count, count)],
                            buffer.at[pl.ds(start, count)],
                            semaphores.at[len(self.copies)],
                        ),
                    )
                )
                start += count
        self.copies = [c for c in self.copies if c[0] < buffer.shape[0]]

    def __getitem__(self, group):
        while self.copies and self.copies[0][0] <= group:
            self.copies.pop(0)[1].wait()
        return self.buffer[group]


class Parts:
    def __init__(self, refs):
        self.refs = refs

    def __getitem__(self, group):
        for ref in self.refs:
            if group < ref.shape[0]:
                return ref[group]
            group -= ref.shape[0]


def order_spec(array):
    return SM if array.dtype == jnp.int32 else pl.BlockSpec(memory_space=pl.ANY)


def call(
    kernel, scalars, arrays, weights, outs, scratch, weight, token=False, after=(), carry=None
):
    single = not isinstance(outs, tuple)
    if single:
        outs = (outs,)
    parts = [p for w in weights for p in w]
    inputs, results = len(scalars) + len(arrays), len(outs)

    def run(*refs):
        first, refs = refs[:inputs], refs[inputs:]
        sources, refs = refs[: len(parts)], refs[len(parts) :]
        rest = refs[len(after) :]
        if carry is not None:
            carried, rest = rest[0], rest[1:]
        results_refs, rest = rest[:results], rest[results:]
        if token:
            rest[0][0] = 0
            rest = rest[1:]
        copy = None
        if carry is not None:
            out, semaphore = rest[0], rest[-1]
            rest = rest[1:-1]
            copy = pltpu.make_async_copy(
                carried.at[pl.ds(carry[1], carry[2])], out, semaphore
            )
            copy.start()
        held, at = [], 0
        for w in weights:
            held.append(Parts(sources[at : at + len(w)]))
            at += len(w)
        kernel(*first, *held, *results_refs, *rest)
        if copy is not None:
            copy.wait()

    out_shape = tuple(outs) + ((jax.ShapeDtypeStruct((1,), jnp.int32),) if token else ())
    out_specs = (VM,) * results + ((SM,) if token else ())
    scratch_shapes = [pltpu.VMEM(shape, f32) for shape in scratch]
    in_specs = [SM] * len(scalars) + [VM] * (len(arrays) + len(parts)) + [order_spec(a) for a in after]
    extra = ()
    if carry is not None:
        array, _, count = carry
        extra = (array,)
        shape = (count,) + array.shape[1:]
        out_shape += (jax.ShapeDtypeStruct(shape, array.dtype),)
        out_specs += (pl.BlockSpec(memory_space=pl.ANY),)
        in_specs.append(pl.BlockSpec(memory_space=pl.ANY))
        scratch_shapes.append(pltpu.SemaphoreType.DMA)
    got = pl.pallas_call(
        run,
        out_shape=out_shape,
        in_specs=in_specs,
        out_specs=out_specs,
        scratch_shapes=scratch_shapes,
        compiler_params=pltpu.CompilerParams(vmem_limit_bytes=VMEM_LIMIT),
        cost_estimate=pl.CostEstimate(
            flops=weight * 10**9, bytes_accessed=8 * 2**20, transcendentals=0
        ),
    )(*scalars, *arrays, *parts, *after, *extra)
    return got[0] if single else got


def drop(kernel, position, **options):
    def run(*refs):
        return kernel(*refs[:position], None, *refs[position:], **options)

    return run


def exchange(value, pairs):
    return lax.ppermute(value, AXES, pairs)


def high_half(rows):
    return 1 - (rows & 1), rows >> 1


def body(
    right_side, ghost_rows, cols_one, diag_one, offd_one, prol_one, agg_one, cols_two, diag_two,
    offd_two, prol_two, agg_two, cols_three, diag_three, offd_three,
):
    blocks = lax.axis_size("grp") * lax.axis_size("dev")
    block = lax.axis_index("grp") * lax.axis_size("dev") + lax.axis_index("dev")
    half = block % 2
    pair = block // 2

    def shift(value, steps):
        return exchange(value, [(s, (s + steps) % blocks) for s in range(blocks)])

    def flip(value, mask):
        return exchange(value, [(s, s ^ mask) for s in range(blocks)])

    left_raw = shift(right_side, 1)
    right_raw = shift(right_side, -1)
    lists = jnp.concatenate([shift(ghost_rows[1], 1), shift(ghost_rows[0], -1)])

    flags_one = jnp.stack([block > 0, block < blocks - 1]).astype(jnp.int32)
    flags_two = jnp.stack([pair > 0, pair < blocks // 2 - 1]).astype(jnp.int32)

    def slots(first, second, base):
        return jnp.concatenate(
            [(1 - (first & 1)) * base + (first >> 1), (second & 1) * base + (second >> 1)]
        )

    def low_slot(rows, base):
        return (rows & 1) * base + (rows >> 1)

    def local_row(rows):
        return (rows + half * HALF) % ROWS

    index_one = slots(cols_one[:, 0], cols_one[:, 1], 72)
    numbers = flip(jnp.concatenate([cols_two.reshape(-1), agg_two]), 1)
    cols_pair = jnp.concatenate([cols_two, numbers[: 2 * HALF].reshape(HALF, 2)], 0)
    cols_pair = (cols_pair // ROWS) * ROWS + local_row(cols_pair % ROWS)
    index_two = slots(cols_pair[:, 0], cols_pair[:, 1], 144)
    index_three = slots(cols_three[:, 0], cols_three[:, 1], COARSE // 2)
    agg_pair = low_slot(jnp.concatenate([agg_two, numbers[2 * HALF :]]), COARSE // 2)
    agg_local = local_row(agg_one)
    lift_index = low_slot(agg_local, 48)

    def paired(prepared):
        return tuple((w,) for w in prepared[:2])

    own_list = ghost_rows.reshape(-1)
    numbers_one = (flags_one, own_list, index_one, lists, agg_local, lift_index)
    numbers_two = (flags_two, index_two, index_three, agg_pair)
    diag_other = flip(diag_two, 1)
    *one_w, _, offd_a = prepare(
        (diag_one, offd_one),
        ROWS,
        after=numbers_one + numbers_two + (left_raw, right_raw),
        carry=(offd_two, 0, 24),
    )
    one_w = paired(one_w)

    v48, v12 = packed(48), packed(12)
    table_one, table_two = (144, 8, 128), (288, 8, 128)
    by_load = (ROWS * 8, 128)

    rhs, r, d, x, to_left, to_right, token = call(
        first_one_kernel,
        (flags_one, own_list, index_one, lists),
        (right_side, left_raw, right_raw),
        one_w,
        (v48, v48, v48, v48, v12, v12),
        (table_one, by_load),
        2,
        token=True,
        after=(diag_other,),
    )
    other_a = prepare((diag_other, flip(offd_a, 1)), 24)
    two_own = prepare((diag_two, offd_two), HALF, after=(token,), carry=(offd_two, 24, 24))
    offd_b = two_own[3]

    def one_turn(d, r, x, to_left, to_right, factors, after=(), token=False):
        from_left, from_right = shift(to_right, 1), shift(to_left, -1)
        return call(
            functools.partial(one_kernel, factors=factors),
            (flags_one, index_one, lists),
            (d, from_left, from_right, r, x),
            one_w,
            (v48, v48, v48, v12, v12),
            (table_one,),
            2,
            after=after,
            token=token,
        )

    r, d, smooth_one, to_left, to_right, token = one_turn(
        d, r, x, to_left, to_right, FACTORS[1], after=(two_own[2], other_a[2]), token=True
    )
    one_p = paired(prepare((prol_one,), ROWS, after=(token,)))
    other_b = prepare((diag_other, flip(offd_b, 1)), 24, start=24)
    two_w = tuple((two_own[k], other_a[k], other_b[k]) for k in range(2))
    part = call(
        restrict_one_kernel,
        (flags_one, index_one, agg_local),
        (d, shift(to_right, 1), shift(to_left, -1), r),
        (*one_w, *one_p),
        v48,
        (table_one,) + ((ROWS, 8, 128),) * 4,
        3,
    )
    rhs_two = combine(part, flip(part, 1))

    def two_turn(d, r, x, factors, scale=False, token=False, after=()):
        from_left, from_right = shift(d, 2), shift(d, -2)
        kernel = functools.partial(two_kernel, factors=factors, scale=scale)
        arrays = [d, from_left, from_right, r]
        if x is None:
            kernel = drop(two_kernel, 6, factors=factors, scale=scale)
        else:
            arrays.append(x)
        return call(
            kernel,
            (flags_two, index_two),
            arrays,
            two_w,
            (v48, v48, v48),
            (table_two,),
            2,
            token=token,
            after=after,
        )

    r, d, x, token = two_turn(rhs_two, rhs_two, None, FACTORS[0], scale=True, token=True)
    three_ready = prepare((diag_three, offd_three), COARSE, after=(token,))
    three_w = paired(three_ready)
    r, d, smooth_two, token = two_turn(
        d, r, x, FACTORS[1], token=True, after=(three_ready[2],)
    )
    two_p = paired(prepare((prol_two,), HALF, after=(token,)))
    two_p_other = paired(prepare((flip(prol_two, 1),), HALF, after=(token,)))
    coarse_rhs = call(
        restrict_two_kernel,
        (flags_two, index_two, agg_two),
        (d, shift(d, 2), shift(d, -2), r),
        (*[w[:1] for w in two_w], *two_p),
        packed(COARSE // 2),
        (table_two,) + ((COARSE, 8, 128),) * 4,
        2,
    )
    for masks in reduce_phases(blocks):
        others = [flip(coarse_rhs, m) for m in masks]
        if len(masks) == 1:
            coarse_rhs = coarse_rhs + others[0]
        else:
            coarse_rhs = (coarse_rhs + others[0]) + (others[1] + others[2])

    coarse_solution, corrected_two = call(
        coarse_kernel,
        (index_three, agg_pair),
        (coarse_rhs, smooth_two),
        (*three_w, *two_p, *two_p_other),
        (jax.ShapeDtypeStruct((COARSE, LOADS * TILE), f32), v48),
        (
            (COARSE, 8, 128),
            (COARSE // 2, 8, 128),
            (COARSE // 2, 8, 128),
            (COARSE // 2, 8, 128),
            (COARSE * 8, 128),
        ),
        4,
    )

    r, d, x = two_turn(corrected_two, rhs_two, corrected_two, None)
    r, d, x = two_turn(d, r, x, FACTORS[0])
    corrected_one, to_left, to_right = call(
        lift_kernel,
        (flags_two, index_two, lift_index, lists),
        (d, shift(d, 2), shift(d, -2), r, x, smooth_one),
        (*two_w, *one_p),
        (v48, v12, v12),
        (table_two, (ROWS, 8, 128)),
        3,
    )

    r, d, x, to_left, to_right = one_turn(
        corrected_one, rhs, corrected_one, to_left, to_right, None
    )
    r, d, x, to_left, to_right = one_turn(d, r, x, to_left, to_right, FACTORS[0])
    solution = call(
        last_one_kernel,
        (flags_one, index_one),
        (d, shift(to_right, 1), shift(to_left, -1), r, x),
        one_w,
        jax.ShapeDtypeStruct((ROWS, LOADS * TILE), f32),
        (table_one, by_load),
        2,
    )
    return solution, coarse_solution


def reduce_phases(blocks):
    if blocks == 256:
        return ((32,), (4,), (8, 16, 24), (64, 128, 192), (1, 2, 3))
    return tuple((1 << bit,) for bit in range(blocks.bit_length() - 1))


def solution(mesh):
    rows = P(AXES, None)
    return jax.shard_map(
        body,
        mesh=mesh,
        in_specs=(
            rows, rows, rows, rows, P(AXES, None, None), rows, P(AXES), rows, rows,
            P(AXES, None, None), rows, P(AXES), P(), P(), P(),
        ),
        out_specs=(rows, P()),
        check_vma=False,
    )
```
